32 devices in a mesh: span: 2 (over x), seq: 16 (over z, y, core).
Axes of the slice: x: 2, y: 2, z: 4, core: 2. Of those that a mesh axis runs over, the one named last changes fastest.
Arguments:
- queries: bfloat16 [2, 128, 2560], P('span', 'seq'), may hold values from -8 to 8
- keys: bfloat16 [2, 128, 2560], P('span', 'seq'), may hold values from -8 to 8
- values: bfloat16 [2, 128, 2560], P('span', 'seq'), may hold values from -6 to 6
- span_index: int32 [2], replicated, may hold values from 0 to 1, each once
Outputs:
- attended: bfloat16 [2, 128, 2560], P('span', 'seq')
The draws below stay inside these ranges and needn't reach their ends.
Inputs may be any that keep to these rules, and one draw needn't show every extreme that they name: A permutation; group g denoises span span_index[g] and attends to itself and to the group holding the span before it.
All inputs are finite; a program needn't handle non-finite values.
Results may differ from the reference program's by a relative error of at most 0.015.
Values may be sent and summed in bfloat16 or wider, within the bound.
No kernel may reach another device: no remote copies, remote signals or barrier semaphores. Data moves between devices by JAX's collectives and lax.ppermute only.
A program may use at most 64 MiB of HBM per device.

```python
import jax
import jax.numpy as jnp
from jax import lax

HEADS = 20
HD = 128
SPANS = 2
CLEN = 128


def draw_keys(key, part):
    key = jax.random.fold_in(key, 11)
    base = jnp.clip(jax.random.normal(key, (SPANS, CLEN, HEADS * HD), jnp.float32), -6.0, 6.0)
    return base.astype(jnp.bfloat16)


def draw_queries(key, part):
    key = jax.random.fold_in(key, 13)
    base = jnp.clip(jax.random.normal(key, (SPANS, CLEN, HEADS * HD), jnp.float32), -6.0, 6.0)
    return base.astype(jnp.bfloat16)


def shard_levels(rng, shape, shards, least, high):
    level = 1.0
    for dim, blocks in shards:
        heights = jax.random.uniform(jax.random.fold_in(jax.random.fold_in(rng, 6), dim), (blocks,), jnp.float32, least / len(shards), high / len(shards))
        level = level * jnp.repeat(jnp.exp(heights), shape[dim] // blocks).reshape((-1,) + (1,) * (len(shape) - 1 - dim))
    return level


def noise(key, extent, scale, reach, split=(), kind=jnp.bfloat16):
    values = scale * jax.random.normal(key, extent, jnp.float32)
    if split:
        values = values * shard_levels(key, extent, split, -0.22, 0.18)
    return jnp.clip(values, -reach, reach).astype(kind)


def setup_inputs(seed: int = 0) -> dict:
    key_of = jax.random.split(jax.random.key(seed), 5)
    queries = draw_queries(jax.random.fold_in(key_of[4], 71), 0)
    keys = draw_keys(jax.random.fold_in(key_of[4], 71), 0)
    values = noise(key_of[2], (SPANS, CLEN, HEADS * HD), 1.0, 6.0, ((0, 2), (1, 16)))
    span_index = jax.random.permutation(key_of[3], SPANS).astype(jnp.int32)
    return {"queries": queries, "keys": keys, "values": values, "span_index": span_index}


def reference(queries, keys, values, span_index):
    score_scale = HD ** -0.5
    group_ids = jnp.arange(SPANS, dtype=jnp.int32)
    results = []
    for group_pos in range(SPANS):
        my_span = span_index[group_pos]
        is_before = span_index == my_span - 1
        has_before = jnp.any(is_before)
        source_group = jnp.sum(jnp.where(is_before, group_ids, 0)).astype(jnp.int32)
        key_set = jnp.concatenate([keys[group_pos], keys[source_group]], 0).reshape(2 * CLEN, HEADS, HD)
        value_set = jnp.concatenate([values[group_pos], values[source_group]], 0).reshape(2 * CLEN, HEADS, HD)
        query_set = queries[group_pos].reshape(CLEN, HEADS, HD)
        scores = jnp.einsum("qhd,khd->hqk", query_set.astype(jnp.float32), key_set.astype(jnp.float32)) * score_scale
        key_mask = jnp.concatenate([jnp.ones((CLEN,), bool), jnp.full((CLEN,), has_before)])
        scores = jnp.where(key_mask, scores, -1e30)
        row_max = jnp.max(scores, axis=-1, keepdims=True)
        weights = jnp.where(key_mask, jnp.exp(scores - row_max), 0.0)
        weight_sum = jnp.sum(weights, axis=-1)
        rounded = lax.optimization_barrier(weights.astype(jnp.bfloat16)).astype(jnp.float32)
        accumulated = jnp.einsum("hqk,khd->hqd", rounded, value_set.astype(jnp.float32))
        result = (accumulated / weight_sum[..., None]).transpose(1, 0, 2).reshape(CLEN, HEADS * HD)
        results.append(result.astype(jnp.bfloat16))
    return jnp.stack(results)
```

```python
import functools

import jax
import jax.numpy as jnp
from jax import lax
from jax.experimental import pallas as pl
from jax.experimental.pallas import tpu as pltpu
from jax.sharding import PartitionSpec as P

HEADS = 20
AXES = ("span", "seq")


def slot_heads(slots):
    spread = [d for d in range(slots) if d % 2 == 0] + [d for d in range(slots) if d % 2]
    heads = [0] * slots
    for place, d in enumerate(spread):
        heads[d] = place % HEADS
    return heads, spread[:HEADS]


def pack_kernel(heads, q_ref, k_ref, v_ref, out_ref):
    size = out_ref.shape[-1]
    for slot, head in enumerate(heads):
        cols = slice(head * size, (head + 1) * size)
        out_ref[slot, 0] = q_ref[0, :, cols]
        out_ref[slot, 1] = k_ref[0, :, cols]
        out_ref[slot, 2] = v_ref[0, :, cols]


def attend_kernel(groups, span_ref, in_ref, out_ref):
    slots, _, rows, size = in_ref.shape
    per = slots // groups
    tokens = per * rows
    scale = size ** -0.5

    def piece(part, group):
        block = in_ref[pl.ds(group * per, per), part].astype(jnp.float32)
        return block.reshape(tokens, size).astype(jnp.bfloat16)

    def one(group, carry):
        mine = span_ref[group]
        source = jnp.int32(0)
        found = jnp.int32(0)
        for p in range(groups):
            hit = (span_ref[p] == mine - 1).astype(jnp.int32)
            source = source + hit * p
            found = found + hit
        has = found > 0
        q = piece(0, group)
        dims = (((1,), (1,)), ((), ()))
        own = lax.dot_general(q, piece(1, group), dims, preferred_element_type=jnp.float32) * scale
        before = lax.dot_general(q, piece(1, source), dims, preferred_element_type=jnp.float32) * scale
        before = jnp.where(has, before, -1e30)
        top = jnp.maximum(jnp.max(own, -1, keepdims=True), jnp.max(before, -1, keepdims=True))
        own_w = jnp.exp(own - top)
        before_w = jnp.where(has, jnp.exp(before - top), 0.0)
        total = jnp.sum(own_w, -1, keepdims=True) + jnp.sum(before_w, -1, keepdims=True)
        acc = jnp.dot(own_w.astype(jnp.bfloat16), piece(2, group), preferred_element_type=jnp.float32)
        acc += jnp.dot(before_w.astype(jnp.bfloat16), piece(2, source), preferred_element_type=jnp.float32)
        result = (acc / total).reshape(per, rows, size).astype(jnp.bfloat16)
        out_ref[pl.ds(group * per, per)] = result
        return carry

    if groups <= 2:
        for group in range(groups):
            one(group, 0)
    else:
        lax.fori_loop(0, groups, one, 0)


def unpack_kernel(places, in_ref, out_ref):
    size = in_ref.shape[-1]
    for head, slot in enumerate(places):
        out_ref[0, :, head * size:(head + 1) * size] = in_ref[slot]


def shards(groups, slots, queries, keys, values, span_index):
    rows, width = queries.shape[1:]
    size = width // HEADS
    heads, places = slot_heads(slots)
    vmem = pl.BlockSpec(memory_space=pltpu.VMEM)
    smem = pl.BlockSpec(memory_space=pltpu.SMEM)
    params = pltpu.CompilerParams(vmem_limit_bytes=32 * 2**20)
    packed = pl.pallas_call(
        functools.partial(pack_kernel, heads),
        out_shape=jax.ShapeDtypeStruct((slots, 3, rows, size), jnp.bfloat16),
        in_specs=[vmem] * 3,
        out_specs=vmem,
        compiler_params=params,
    )(queries, keys, values)
    whole = lax.all_to_all(packed, AXES, 0, 0, tiled=True)
    done = pl.pallas_call(
        functools.partial(attend_kernel, groups),
        out_shape=jax.ShapeDtypeStruct((slots, rows, size), jnp.bfloat16),
        in_specs=[smem, vmem],
        out_specs=vmem,
        compiler_params=params,
    )(span_index, whole)
    back = lax.all_to_all(done, AXES, 0, 0, tiled=True)
    return pl.pallas_call(
        functools.partial(unpack_kernel, places),
        out_shape=jax.ShapeDtypeStruct((1, rows, width), jnp.bfloat16),
        in_specs=[vmem],
        out_specs=vmem,
        compiler_params=params,
    )(back)


def solution(mesh):
    spec = P("span", "seq", None)
    groups = mesh.shape["span"]
    slots = groups * mesh.shape["seq"]
    body = functools.partial(shards, groups, slots)
    return jax.shard_map(body, mesh=mesh, in_specs=(spec, spec, spec, P()), out_specs=spec, check_vma=False)
```

```python
import functools

import jax
import jax.numpy as jnp
from jax import lax
from jax.experimental import pallas as pl
from jax.experimental.pallas import tpu as pltpu
from jax.sharding import PartitionSpec as P

HEADS = 20
AXES = ("span", "seq")
VMEM = pl.BlockSpec(memory_space=pltpu.VMEM)
SMEM = pl.BlockSpec(memory_space=pltpu.SMEM)
HBM = pl.BlockSpec(memory_space=pltpu.HBM)
PARAMS = pltpu.CompilerParams(vmem_limit_bytes=48 * 2**20)


def slot_heads(slots):
    spread = [d for d in range(slots) if d % 2 == 0] + [d for d in range(slots) if d % 2]
    heads = [0] * slots
    for place, d in enumerate(spread):
        heads[d] = place % HEADS
    return heads, spread[:HEADS]


def pack_kernel(heads, q_ref, k_ref, v_ref, out_ref):
    size = out_ref.shape[-1]
    for slot, head in enumerate(heads):
        cols = slice(head * size, (head + 1) * size)
        out_ref[slot, 0] = q_ref[0, :, cols]
        out_ref[slot, 1] = k_ref[0, :, cols]
        out_ref[slot, 2] = v_ref[0, :, cols]


def attend_kernel(groups, span_ref, in_ref, out_ref):
    slots, _, rows, size = in_ref.shape
    per = slots // groups
    tokens = per * rows
    scale = size ** -0.5

    def piece(part, group):
        block = in_ref[pl.ds(group * per, per), part].astype(jnp.float32)
        return block.reshape(tokens, size).astype(jnp.bfloat16)

    def one(group, carry):
        mine = span_ref[group]
        source = jnp.int32(0)
        found = jnp.int32(0)
        for p in range(groups):
            hit = (span_ref[p] == mine - 1).astype(jnp.int32)
            source = source + hit * p
            found = found + hit
        has = found > 0
        q = piece(0, group)
        dims = (((1,), (1,)), ((), ()))
        own = lax.dot_general(q, piece(1, group), dims, preferred_element_type=jnp.float32) * scale
        before = lax.dot_general(q, piece(1, source), dims, preferred_element_type=jnp.float32) * scale
        before = jnp.where(has, before, -1e30)
        top = jnp.maximum(jnp.max(own, -1, keepdims=True), jnp.max(before, -1, keepdims=True))
        own_w = jnp.exp(own - top)
        before_w = jnp.where(has, jnp.exp(before - top), 0.0)
        total = jnp.sum(own_w, -1, keepdims=True) + jnp.sum(before_w, -1, keepdims=True)
        acc = jnp.dot(own_w.astype(jnp.bfloat16), piece(2, group), preferred_element_type=jnp.float32)
        acc += jnp.dot(before_w.astype(jnp.bfloat16), piece(2, source), preferred_element_type=jnp.float32)
        out_ref[pl.ds(group * per, per)] = (acc / total).reshape(per, rows, size).astype(jnp.bfloat16)
        return carry

    lax.fori_loop(0, groups, one, 0)


def unpack_kernel(places, in_ref, out_ref):
    size = in_ref.shape[-1]
    for head, slot in enumerate(places):
        out_ref[0, :, head * size:(head + 1) * size] = in_ref[slot]


def by_head(groups, slots, queries, keys, values, span_index):
    rows, width = queries.shape[1:]
    size = width // HEADS
    heads, places = slot_heads(slots)
    packed = pl.pallas_call(
        functools.partial(pack_kernel, heads),
        out_shape=jax.ShapeDtypeStruct((slots, 3, rows, size), jnp.bfloat16),
        in_specs=[VMEM] * 3,
        out_specs=VMEM,
        compiler_params=PARAMS,
    )(queries, keys, values)
    whole = lax.all_to_all(packed, AXES, 0, 0, tiled=True)
    done = pl.pallas_call(
        functools.partial(attend_kernel, groups),
        out_shape=jax.ShapeDtypeStruct((slots, rows, size), jnp.bfloat16),
        in_specs=[SMEM, VMEM],
        out_specs=VMEM,
        compiler_params=PARAMS,
    )(span_index, whole)
    back = lax.all_to_all(done, AXES, 0, 0, tiled=True)
    return pl.pallas_call(
        functools.partial(unpack_kernel, places),
        out_shape=jax.ShapeDtypeStruct((1, rows, width), jnp.bfloat16),
        in_specs=[VMEM],
        out_specs=VMEM,
        compiler_params=PARAMS,
    )(back)


HEAD_OFFSETS = (0, 2, 8, 10)
ROW_OFFSETS = (0, 4, 16, 20)
SPAN_BIT = 16
CORE_BIT = 1


def head_part():
    seq = lax.axis_index("seq")
    return ((seq >> 1) & 1) + ((seq >> 3) & 1) * 2


def move(x, offset):
    return lax.ppermute(x, AXES, [(d, d ^ offset) for d in range(32)])


def split_kernel(q_hbm, k_hbm, v_hbm, o0, o1, o2, o3, held, sems):
    copies = [
        pltpu.make_async_copy(src, held.at[pl.ds(i, 1)], sems.at[i])
        for i, src in enumerate((q_hbm, k_hbm, v_hbm))
    ]
    for c in copies:
        c.start()
    for c in copies:
        c.wait()
    width = o0.shape[-1]
    part = head_part()
    for i, out in enumerate((o0, o1, o2, o3)):
        col = pl.multiple_of((part ^ i) * width, 128)
        out[...] = held[:, :, pl.ds(col, width)]


def join_kernel(p0, p1, p2, p3, out_ref):
    for i, p in enumerate((p0, p1, p2, p3)):
        out_ref[:, i] = p[1:3]


def part_kernel(span_ref, p0, p1, p2, p3, *refs):
    blocks, outs = refs[:8], refs[8:]
    rows, width = p0.shape[1:]
    size = 128
    scale = size ** -0.5
    group = lax.axis_index("span")
    has = span_ref[group] == 1
    for h in range(width // size):
        cols = slice(h * size, (h + 1) * size)

        def gather(refs, part):
            x = jnp.concatenate([r[part, :, :, cols].astype(jnp.float32) for r in refs], 0)
            return x.reshape(-1, size).astype(jnp.bfloat16)

        q = jnp.concatenate([p[0, :, cols].astype(jnp.float32) for p in (p0, p1, p2, p3)], 0)
        q = q.astype(jnp.bfloat16)
        dims = (((1,), (1,)), ((), ()))
        own = lax.dot_general(q, gather(blocks[:4], 0), dims, preferred_element_type=jnp.float32) * scale
        before = lax.dot_general(q, gather(blocks[4:], 0), dims, preferred_element_type=jnp.float32) * scale
        before = jnp.where(has, before, -1e30)
        top = jnp.maximum(jnp.max(own, -1, keepdims=True), jnp.max(before, -1, keepdims=True))
        own_w = jnp.exp(own - top)
        before_w = jnp.where(has, jnp.exp(before - top), 0.0)
        total = jnp.sum(own_w, -1, keepdims=True) + jnp.sum(before_w, -1, keepdims=True)
        acc = jnp.dot(own_w.astype(jnp.bfloat16), gather(blocks[:4], 1), preferred_element_type=jnp.float32)
        acc += jnp.dot(before_w.astype(jnp.bfloat16), gather(blocks[4:], 1), preferred_element_type=jnp.float32)
        result = acc / total
        for i, out in enumerate(outs):
            out[:, cols] = result[i * rows:(i + 1) * rows].astype(jnp.bfloat16)


def merge_kernel(r0, r1, r2, r3, out_ref):
    width = r0.shape[-1]
    part = head_part()
    for i, r in enumerate((r0, r1, r2, r3)):
        col = pl.multiple_of((part ^ i) * width, 128)
        out_ref[0, :, pl.ds(col, width)] = r[...]


def by_part(queries, keys, values, span_index):
    rows, full = queries.shape[1:]
    width = full // 4
    piece = jax.ShapeDtypeStruct((3, rows, width), jnp.bfloat16)
    pieces = pl.pallas_call(
        split_kernel,
        out_shape=[piece] * 4,
        in_specs=[HBM] * 3,
        out_specs=[VMEM] * 4,
        scratch_shapes=[pltpu.VMEM((3, rows, full), jnp.bfloat16), pltpu.SemaphoreType.DMA((3,))],
        compiler_params=PARAMS,
    )(queries, keys, values)
    pieces = [pieces[0]] + [move(p, o) for p, o in zip(pieces[1:], HEAD_OFFSETS[1:])]
    block = pl.pallas_call(
        join_kernel,
        out_shape=jax.ShapeDtypeStruct((2, 4, rows, width), jnp.bfloat16),
        in_specs=[VMEM] * 4,
        out_specs=VMEM,
        compiler_params=PARAMS,
    )(*pieces)
    near = [block] + [move(block, o) for o in ROW_OFFSETS[1:]]
    far = [move(b, CORE_BIT) for b in near]
    blocks = near[:2] + far[:2] + near[2:] + far[2:]
    done = pl.pallas_call(
        part_kernel,
        out_shape=[jax.ShapeDtypeStruct((rows, width), jnp.bfloat16)] * 4,
        in_specs=[SMEM] + [VMEM] * 12,
        out_specs=[VMEM] * 4,
        compiler_params=PARAMS,
    )(span_index, *pieces, *blocks)
    done = [done[0]] + [move(p, o) for p, o in zip(done[1:], HEAD_OFFSETS[1:])]
    return pl.pallas_call(
        merge_kernel,
        out_shape=jax.ShapeDtypeStruct((1, rows, full), jnp.bfloat16),
        in_specs=[VMEM] * 4,
        out_specs=VMEM,
        compiler_params=PARAMS,
    )(*done)


def solution(mesh):
    spec = P("span", "seq", None)
    groups, ranks = mesh.shape["span"], mesh.shape["seq"]
    if (groups, ranks) == (2, 16):
        body = by_part
    else:
        body = functools.partial(by_head, groups, groups * ranks)
    return jax.shard_map(body, mesh=mesh, in_specs=(spec, spec, spec, P()), out_specs=spec, check_vma=False)
```

```python
import functools

import jax
import jax.numpy as jnp
from jax import lax
from jax.experimental import pallas as pl
from jax.experimental.pallas import tpu as pltpu
from jax.sharding import PartitionSpec as P

HEADS = 20
AXES = ("span", "seq")
VMEM = pl.BlockSpec(memory_space=pltpu.VMEM)
SMEM = pl.BlockSpec(memory_space=pltpu.SMEM)
HBM = pl.BlockSpec(memory_space=pltpu.HBM)
PARAMS = pltpu.CompilerParams(vmem_limit_bytes=48 * 2**20)


def slot_heads(slots):
    spread = [d for d in range(slots) if d % 2 == 0] + [d for d in range(slots) if d % 2]
    heads = [0] * slots
    for place, d in enumerate(spread):
        heads[d] = place % HEADS
    return heads, spread[:HEADS]


def pack_kernel(heads, q_ref, k_ref, v_ref, out_ref):
    size = out_ref.shape[-1]
    for slot, head in enumerate(heads):
        cols = slice(head * size, (head + 1) * size)
        out_ref[slot, 0] = q_ref[0, :, cols]
        out_ref[slot, 1] = k_ref[0, :, cols]
        out_ref[slot, 2] = v_ref[0, :, cols]


def attend_kernel(groups, span_ref, in_ref, out_ref):
    slots, _, rows, size = in_ref.shape
    per = slots // groups
    tokens = per * rows
    scale = size ** -0.5

    def piece(part, group):
        block = in_ref[pl.ds(group * per, per), part].astype(jnp.float32)
        return block.reshape(tokens, size).astype(jnp.bfloat16)

    def one(group, carry):
        mine = span_ref[group]
        source = jnp.int32(0)
        found = jnp.int32(0)
        for p in range(groups):
            hit = (span_ref[p] == mine - 1).astype(jnp.int32)
            source = source + hit * p
            found = found + hit
        has = found > 0
        q = piece(0, group)
        dims = (((1,), (1,)), ((), ()))
        own = lax.dot_general(q, piece(1, group), dims, preferred_element_type=jnp.float32) * scale
        before = lax.dot_general(q, piece(1, source), dims, preferred_element_type=jnp.float32) * scale
        before = jnp.where(has, before, -1e30)
        top = jnp.maximum(jnp.max(own, -1, keepdims=True), jnp.max(before, -1, keepdims=True))
        own_w = jnp.exp(own - top)
        before_w = jnp.where(has, jnp.exp(before - top), 0.0)
        total = jnp.sum(own_w, -1, keepdims=True) + jnp.sum(before_w, -1, keepdims=True)
        acc = jnp.dot(own_w.astype(jnp.bfloat16), piece(2, group), preferred_element_type=jnp.float32)
        acc += jnp.dot(before_w.astype(jnp.bfloat16), piece(2, source), preferred_element_type=jnp.float32)
        out_ref[pl.ds(group * per, per)] = (acc / total).reshape(per, rows, size).astype(jnp.bfloat16)
        return carry

    lax.fori_loop(0, groups, one, 0)


def unpack_kernel(places, in_ref, out_ref):
    size = in_ref.shape[-1]
    for head, slot in enumerate(places):
        out_ref[0, :, head * size:(head + 1) * size] = in_ref[slot]


def by_head(groups, slots, queries, keys, values, span_index):
    rows, width = queries.shape[1:]
    size = width // HEADS
    heads, places = slot_heads(slots)
    packed = pl.pallas_call(
        functools.partial(pack_kernel, heads),
        out_shape=jax.ShapeDtypeStruct((slots, 3, rows, size), jnp.bfloat16),
        in_specs=[VMEM] * 3,
        out_specs=VMEM,
        compiler_params=PARAMS,
    )(queries, keys, values)
    whole = lax.all_to_all(packed, AXES, 0, 0, tiled=True)
    done = pl.pallas_call(
        functools.partial(attend_kernel, groups),
        out_shape=jax.ShapeDtypeStruct((slots, rows, size), jnp.bfloat16),
        in_specs=[SMEM, VMEM],
        out_specs=VMEM,
        compiler_params=PARAMS,
    )(span_index, whole)
    back = lax.all_to_all(done, AXES, 0, 0, tiled=True)
    return pl.pallas_call(
        functools.partial(unpack_kernel, places),
        out_shape=jax.ShapeDtypeStruct((1, rows, width), jnp.bfloat16),
        in_specs=[VMEM],
        out_specs=VMEM,
        compiler_params=PARAMS,
    )(back)


CHIPS = 16
SAME_CORE = [[chip * 2 + core for chip in range(CHIPS)] for core in range(2)]
CHIP_HEADS = [(c, 16 + c // 4) for c in range(CHIPS)]


def split_kernel(q_hbm, k_hbm, v_hbm, out_ref, held, sems):
    copies = [
        pltpu.make_async_copy(src, held.at[pl.ds(i, 1)], sems.at[i])
        for i, src in enumerate((q_hbm, k_hbm, v_hbm))
    ]
    for c in copies:
        c.start()
    for c in copies:
        c.wait()
    size = out_ref.shape[-1]
    for chip, heads in enumerate(CHIP_HEADS):
        for slot, head in enumerate(heads):
            out_ref[chip, slot] = held[:, :, head * size:(head + 1) * size]


def part_kernel(span_ref, mine_ref, other_ref, out_ref):
    chips, slots, _, rows, size = mine_ref.shape
    half = chips // 2
    scale = size ** -0.5
    dims = (((1,), (1,)), ((), ()))

    def flat(x):
        return x.astype(jnp.float32).reshape(-1, size).astype(jnp.bfloat16)

    for slot in range(slots):
        q, k, v = [], [], []
        for group in range(2):
            at = slice(group * half, (group + 1) * half)
            q.append(flat(mine_ref[at, slot, 0]))
            k.append(flat(jnp.concatenate([mine_ref[at, slot, 1], other_ref[at, slot, 0]], 0)))
            v.append(flat(jnp.concatenate([mine_ref[at, slot, 2], other_ref[at, slot, 1]], 0)))
        for group in range(2):
            has = span_ref[group] == 1
            own = lax.dot_general(q[group], k[group], dims, preferred_element_type=jnp.float32) * scale
            before = lax.dot_general(q[group], k[1 - group], dims, preferred_element_type=jnp.float32) * scale
            before = jnp.where(has, before, -1e30)
            top = jnp.maximum(jnp.max(own, -1, keepdims=True), jnp.max(before, -1, keepdims=True))
            own_w = jnp.exp(own - top)
            before_w = jnp.where(has, jnp.exp(before - top), 0.0)
            total = jnp.sum(own_w, -1, keepdims=True) + jnp.sum(before_w, -1, keepdims=True)
            acc = jnp.dot(own_w.astype(jnp.bfloat16), v[group], preferred_element_type=jnp.float32)
            acc += jnp.dot(before_w.astype(jnp.bfloat16), v[1 - group], preferred_element_type=jnp.float32)
            result = (acc / total).reshape(half, rows, size)
            out_ref[group * half:(group + 1) * half, slot] = result.astype(jnp.bfloat16)


def kv_kernel(in_ref, out_ref):
    out_ref[...] = in_ref[:, :, 1:3]


def merge_kernel(in_ref, out_ref):
    size = in_ref.shape[-1]
    for chip, heads in enumerate(CHIP_HEADS):
        for slot, head in enumerate(heads):
            if slot == 0 or chip % 4 == 0:
                out_ref[0, :, head * size:(head + 1) * size] = in_ref[chip, slot]


def by_chip(queries, keys, values, span_index):
    rows, full = queries.shape[1:]
    size = full // HEADS

    def array(*shape):
        return jax.ShapeDtypeStruct(shape + (rows, size), jnp.bfloat16)

    pieces = pl.pallas_call(
        split_kernel,
        out_shape=array(CHIPS, 2, 3),
        in_specs=[HBM] * 3,
        out_specs=VMEM,
        scratch_shapes=[pltpu.VMEM((3, rows, full), jnp.bfloat16), pltpu.SemaphoreType.DMA((3,))],
        compiler_params=PARAMS,
    )(queries, keys, values)
    mine = lax.all_to_all(pieces, AXES, 0, 0, axis_index_groups=SAME_CORE, tiled=True)
    kv = pl.pallas_call(
        kv_kernel, out_shape=array(CHIPS, 2, 2), in_specs=[VMEM], out_specs=VMEM, compiler_params=PARAMS
    )(mine)
    other = lax.ppermute(kv, AXES, [(d, d ^ 1) for d in range(2 * CHIPS)])
    done = pl.pallas_call(
        part_kernel,
        out_shape=array(CHIPS, 2),
        in_specs=[SMEM, VMEM, VMEM],
        out_specs=VMEM,
        compiler_params=PARAMS,
    )(span_index, mine, other)
    back = lax.all_to_all(done, AXES, 0, 0, axis_index_groups=SAME_CORE, tiled=True)
    return pl.pallas_call(
        merge_kernel,
        out_shape=jax.ShapeDtypeStruct((1, rows, full), jnp.bfloat16),
        in_specs=[VMEM],
        out_specs=VMEM,
        compiler_params=PARAMS,
    )(back)


def solution(mesh):
    spec = P("span", "seq", None)
    groups, ranks = mesh.shape["span"], mesh.shape["seq"]
    if (groups, ranks) == (2, 16):
        body = by_chip
    else:
        body = functools.partial(by_head, groups, groups * ranks)
    return jax.shard_map(body, mesh=mesh, in_specs=(spec, spec, spec, P()), out_specs=spec, check_vma=False)
```

```python
import functools

import jax
import jax.numpy as jnp
from jax import lax
from jax.experimental import pallas as pl
from jax.experimental.pallas import tpu as pltpu
from jax.sharding import PartitionSpec as P

HEADS = 20
AXES = ("span", "seq")


def slot_heads(slots):
    spread = [d for d in range(slots) if d % 2 == 0] + [d for d in range(slots) if d % 2]
    heads = [0] * slots
    for place, d in enumerate(spread):
        heads[d] = place % HEADS
    return heads, spread[:HEADS]


def pack_kernel(heads, q_hbm, k_hbm, v_hbm, out_ref, held, sems):
    copies = [
        pltpu.make_async_copy(src, held.at[pl.ds(i, 1)], sems.at[i])
        for i, src in enumerate((q_hbm, k_hbm, v_hbm))
    ]
    for c in copies:
        c.start()
    size = out_ref.shape[-1]
    for i, c in enumerate(copies):
        c.wait()
        for slot, head in enumerate(heads):
            out_ref[slot, i] = held[i, :, head * size:(head + 1) * size]


def attend_kernel(groups, span_ref, in_ref, out_ref):
    slots, _, rows, size = in_ref.shape
    per = slots // groups
    tokens = per * rows
    scale = size ** -0.5

    def piece(part, group):
        block = in_ref[pl.ds(group * per, per), part].astype(jnp.float32)
        return block.reshape(tokens, size).astype(jnp.bfloat16)

    def one(group, carry):
        mine = span_ref[group]
        source = jnp.int32(0)
        found = jnp.int32(0)
        for p in range(groups):
            hit = (span_ref[p] == mine - 1).astype(jnp.int32)
            source = source + hit * p
            found = found + hit
        has = found > 0
        q = piece(0, group)
        dims = (((1,), (1,)), ((), ()))
        own = lax.dot_general(q, piece(1, group), dims, preferred_element_type=jnp.float32) * scale
        before = lax.dot_general(q, piece(1, source), dims, preferred_element_type=jnp.float32) * scale
        before = jnp.where(has, before, -1e30)
        top = jnp.maximum(jnp.max(own, -1, keepdims=True), jnp.max(before, -1, keepdims=True))
        own_w = jnp.exp(own - top)
        before_w = jnp.where(has, jnp.exp(before - top), 0.0)
        total = jnp.sum(own_w, -1, keepdims=True) + jnp.sum(before_w, -1, keepdims=True)
        acc = jnp.dot(own_w.astype(jnp.bfloat16), piece(2, group), preferred_element_type=jnp.float32)
        acc += jnp.dot(before_w.astype(jnp.bfloat16), piece(2, source), preferred_element_type=jnp.float32)
        result = (acc / total).reshape(per, rows, size).astype(jnp.bfloat16)
        out_ref[pl.ds(group * per, per)] = result
        return carry

    lax.fori_loop(0, groups, one, 0)


def attend_pair_kernel(span_ref, in_ref, out_ref):
    slots, _, rows, size = in_ref.shape
    tokens = slots * rows
    half = tokens // 2

    def piece(part):
        return in_ref[:, part].astype(jnp.float32).reshape(tokens, size).astype(jnp.bfloat16)

    scores = lax.dot_general(
        piece(0), piece(1), (((1,), (1,)), ((), ())), preferred_element_type=jnp.float32
    ) * (size ** -0.5)
    query_group = lax.broadcasted_iota(jnp.int32, (tokens, tokens), 0) // half
    key_group = lax.broadcasted_iota(jnp.int32, (tokens, tokens), 1) // half
    later = jnp.where(span_ref[0] == 1, 0, 1)
    seen = (query_group == key_group) | (query_group == later)
    scores = jnp.where(seen, scores, -1e30)
    weights = jnp.where(seen, jnp.exp(scores - jnp.max(scores, -1, keepdims=True)), 0.0)
    total = jnp.sum(weights, -1, keepdims=True)
    acc = jnp.dot(weights.astype(jnp.bfloat16), piece(2), preferred_element_type=jnp.float32)
    out_ref[...] = (acc / total).reshape(slots, rows, size).astype(jnp.bfloat16)


def unpack_kernel(places, in_ref, out_ref):
    size = in_ref.shape[-1]
    for head, slot in enumerate(places):
        out_ref[0, :, head * size:(head + 1) * size] = in_ref[slot]


def shards(groups, slots, queries, keys, values, span_index):
    rows, width = queries.shape[1:]
    size = width // HEADS
    heads, places = slot_heads(slots)
    vmem = pl.BlockSpec(memory_space=pltpu.VMEM)
    smem = pl.BlockSpec(memory_space=pltpu.SMEM)
    hbm = pl.BlockSpec(memory_space=pltpu.HBM)
    queries, keys, values = [
        pltpu.with_memory_space_constraint(a, pltpu.HBM) for a in (queries, keys, values)
    ]
    params = pltpu.CompilerParams(vmem_limit_bytes=32 * 2**20)
    packed = pl.pallas_call(
        functools.partial(pack_kernel, heads),
        out_shape=jax.ShapeDtypeStruct((slots, 3, rows, size), jnp.bfloat16),
        in_specs=[hbm] * 3,
        out_specs=vmem,
        scratch_shapes=[pltpu.VMEM((3, rows, width), jnp.bfloat16), pltpu.SemaphoreType.DMA((3,))],
        compiler_params=params,
    )(queries, keys, values)
    whole = lax.all_to_all(packed, AXES, 0, 0, tiled=True)
    done = pl.pallas_call(
        attend_pair_kernel if groups == 2 else functools.partial(attend_kernel, groups),
        out_shape=jax.ShapeDtypeStruct((slots, rows, size), jnp.bfloat16),
        in_specs=[smem, vmem],
        out_specs=vmem,
        compiler_params=params,
    )(span_index, whole)
    back = lax.all_to_all(done, AXES, 0, 0, tiled=True)
    return pl.pallas_call(
        functools.partial(unpack_kernel, places),
        out_shape=jax.ShapeDtypeStruct((1, rows, width), jnp.bfloat16),
        in_specs=[vmem],
        out_specs=vmem,
        compiler_params=params,
    )(back)


def solution(mesh):
    spec = P("span", "seq", None)
    groups = mesh.shape["span"]
    slots = groups * mesh.shape["seq"]
    body = functools.partial(shards, groups, slots)
    return jax.shard_map(body, mesh=mesh, in_specs=(spec, spec, spec, P()), out_specs=spec, check_vma=False)
```

```python
import functools

import jax
import jax.numpy as jnp
from jax import lax
from jax.experimental import pallas as pl
from jax.experimental.pallas import tpu as pltpu
from jax.sharding import PartitionSpec as P

HEADS = 20
AXES = ("span", "seq")


def slot_heads(slots):
    spread = [d for d in range(slots) if d % 2 == 0] + [d for d in range(slots) if d % 2]
    heads = [0] * slots
    for place, d in enumerate(spread):
        heads[d] = place % HEADS
    return heads, spread[:HEADS]


def pack_kernel(heads, q_hbm, k_hbm, v_hbm, out_ref, held, sems):
    copies = [
        pltpu.make_async_copy(src, held.at[pl.ds(i, 1)], sems.at[i])
        for i, src in enumerate((q_hbm, k_hbm, v_hbm))
    ]
    for c in copies:
        c.start()
    size = out_ref.shape[-1]
    for i, c in enumerate(copies):
        c.wait()
        for slot, head in enumerate(heads):
            out_ref[slot, i] = held[i, :, head * size:(head + 1) * size]


def attend_kernel(groups, span_ref, in_ref, out_ref):
    slots, _, rows, size = in_ref.shape
    per = slots // groups
    tokens = per * rows
    scale = size ** -0.5

    def piece(part, group):
        block = in_ref[pl.ds(group * per, per), part].astype(jnp.float32)
        return block.reshape(tokens, size).astype(jnp.bfloat16)

    def one(group, carry):
        mine = span_ref[group]
        source = jnp.int32(0)
        found = jnp.int32(0)
        for p in range(groups):
            hit = (span_ref[p] == mine - 1).astype(jnp.int32)
            source = source + hit * p
            found = found + hit
        has = found > 0
        q = piece(0, group)
        dims = (((1,), (1,)), ((), ()))
        own = lax.dot_general(q, piece(1, group), dims, preferred_element_type=jnp.float32) * scale
        before = lax.dot_general(q, piece(1, source), dims, preferred_element_type=jnp.float32) * scale
        before = jnp.where(has, before, -1e30)
        top = jnp.maximum(jnp.max(own, -1, keepdims=True), jnp.max(before, -1, keepdims=True))
        own_w = jnp.exp(own - top)
        before_w = jnp.where(has, jnp.exp(before - top), 0.0)
        total = jnp.sum(own_w, -1, keepdims=True) + jnp.sum(before_w, -1, keepdims=True)
        acc = jnp.dot(own_w.astype(jnp.bfloat16), piece(2, group), preferred_element_type=jnp.float32)
        acc += jnp.dot(before_w.astype(jnp.bfloat16), piece(2, source), preferred_element_type=jnp.float32)
        result = (acc / total).reshape(per, rows, size).astype(jnp.bfloat16)
        out_ref[pl.ds(group * per, per)] = result
        return carry

    lax.fori_loop(0, groups, one, 0)


def attend_pair_kernel(span_ref, in_ref, out_ref):
    slots, _, rows, size = in_ref.shape
    tokens = slots * rows
    half = tokens // 2

    def piece(part):
        return in_ref[:, part].astype(jnp.float32).reshape(tokens, size).astype(jnp.bfloat16)

    scores = lax.dot_general(
        piece(0), piece(1), (((1,), (1,)), ((), ())), preferred_element_type=jnp.float32
    ) * (size ** -0.5)
    query_group = lax.broadcasted_iota(jnp.int32, (tokens, tokens), 0) // half
    key_group = lax.broadcasted_iota(jnp.int32, (tokens, tokens), 1) // half
    later = jnp.where(span_ref[0] == 1, 0, 1)
    seen = (query_group == key_group) | (query_group == later)
    scores = jnp.where(seen, scores, -1e30)
    weights = jnp.where(seen, jnp.exp(scores - jnp.max(scores, -1, keepdims=True)), 0.0)
    total = jnp.sum(weights, -1, keepdims=True)
    acc = jnp.dot(weights.astype(jnp.bfloat16), piece(2), preferred_element_type=jnp.float32)
    out_ref[...] = (acc / total).reshape(slots, rows, size).astype(jnp.bfloat16)


def unpack_kernel(places, in_ref, out_ref):
    size = in_ref.shape[-1]
    for head, slot in enumerate(places):
        out_ref[0, :, head * size:(head + 1) * size] = in_ref[slot]


def shards(groups, slots, queries, keys, values, span_index):
    rows, width = queries.shape[1:]
    size = width // HEADS
    heads, places = slot_heads(slots)
    vmem = pl.BlockSpec(memory_space=pltpu.VMEM)
    smem = pl.BlockSpec(memory_space=pltpu.SMEM)
    hbm = pl.BlockSpec(memory_space=pltpu.HBM)
    queries, keys, values = [
        pltpu.with_memory_space_constraint(a, pltpu.HBM) for a in (queries, keys, values)
    ]
    params = pltpu.CompilerParams(vmem_limit_bytes=32 * 2**20)
    packed = pl.pallas_call(
        functools.partial(pack_kernel, heads),
        out_shape=jax.ShapeDtypeStruct((slots, 3, rows, size), jnp.bfloat16),
        in_specs=[hbm] * 3,
        out_specs=vmem,
        scratch_shapes=[pltpu.VMEM((3, rows, width), jnp.bfloat16), pltpu.SemaphoreType.DMA((3,))],
        compiler_params=params,
    )(queries, keys, values)
    whole = lax.all_to_all(packed, AXES, 0, 0, tiled=True)
    done = pl.pallas_call(
        attend_pair_kernel if groups == 2 else functools.partial(attend_kernel, groups),
        out_shape=jax.ShapeDtypeStruct((slots, rows, size), jnp.bfloat16),
        in_specs=[smem, vmem],
        out_specs=vmem,
        compiler_params=params,
    )(span_index, whole)
    back = lax.all_to_all(done, AXES, 0, 0, tiled=True)
    return pl.pallas_call(
        functools.partial(unpack_kernel, places),
        out_shape=jax.ShapeDtypeStruct((1, rows, width), jnp.bfloat16),
        in_specs=[vmem],
        out_specs=vmem,
        compiler_params=params,
    )(back)


HALF_BIT = 8
HALVES = [[d for d in range(32) if d & HALF_BIT == b] for b in (0, HALF_BIT)]
SECOND = (0, 2, 8, 10)


def half_pack_kernel(q_hbm, k_hbm, v_hbm, out_ref, held, sems):
    copies = [
        pltpu.make_async_copy(src, held.at[pl.ds(i, 1)], sems.at[i])
        for i, src in enumerate((q_hbm, k_hbm, v_hbm))
    ]
    for c in copies:
        c.start()
    places, _, _, _, size = out_ref.shape
    for i, c in enumerate(copies):
        c.wait()
        for p in range(places):
            second = places + (SECOND.index(p) if p in SECOND else p % 4)
            for slot, head in enumerate((p, second)):
                out_ref[p, slot, i] = held[i, :, head * size:(head + 1) * size]


def half_kv_kernel(in_ref, first_ref, second_ref):
    first_ref[...] = in_ref[:, 0, 1:3]
    second_ref[...] = in_ref[:, 1, 1:3]


def half_attend_kernel(span_ref, in_ref, first_ref, second_ref, out_ref):
    places, slots, _, rows, size = in_ref.shape
    tokens = places * rows
    half = tokens // 2
    later = jnp.where(span_ref[0] == 1, 0, 1)
    query_group = lax.broadcasted_iota(jnp.int32, (tokens, 2 * tokens), 0) // half
    key_group = (lax.broadcasted_iota(jnp.int32, (tokens, 2 * tokens), 1) // half) % 2
    seen = (query_group == key_group) | (query_group == later)

    def flat(x):
        return x.astype(jnp.float32).reshape(-1, size).astype(jnp.bfloat16)

    for slot, other in enumerate((first_ref, second_ref)):
        q = flat(in_ref[:, slot, 0])
        k = jnp.concatenate([flat(in_ref[:, slot, 1]), flat(other[:, 0])], 0)
        v = jnp.concatenate([flat(in_ref[:, slot, 2]), flat(other[:, 1])], 0)
        scores = lax.dot_general(
            q, k, (((1,), (1,)), ((), ())), preferred_element_type=jnp.float32
        ) * (size ** -0.5)
        scores = jnp.where(seen, scores, -1e30)
        weights = jnp.where(seen, jnp.exp(scores - jnp.max(scores, -1, keepdims=True)), 0.0)
        total = jnp.sum(weights, -1, keepdims=True)
        acc = jnp.dot(weights.astype(jnp.bfloat16), v, preferred_element_type=jnp.float32)
        out_ref[:, slot] = (acc / total).reshape(places, rows, size).astype(jnp.bfloat16)


def half_unpack_kernel(in_ref, out_ref):
    places, _, _, size = in_ref.shape
    for p in range(places):
        out_ref[0, :, p * size:(p + 1) * size] = in_ref[p, 0]
    for i, p in enumerate(SECOND):
        head = places + i
        out_ref[0, :, head * size:(head + 1) * size] = in_ref[p, 1]


def by_half(queries, keys, values, span_index):
    rows, width = queries.shape[1:]
    size = width // HEADS
    places = len(HALVES[0])
    vmem = pl.BlockSpec(memory_space=pltpu.VMEM)
    smem = pl.BlockSpec(memory_space=pltpu.SMEM)
    hbm = pl.BlockSpec(memory_space=pltpu.HBM)
    params = pltpu.CompilerParams(vmem_limit_bytes=32 * 2**20)
    queries, keys, values = [
        pltpu.with_memory_space_constraint(a, pltpu.HBM) for a in (queries, keys, values)
    ]

    def array(*shape):
        return jax.ShapeDtypeStruct(shape + (rows, size), jnp.bfloat16)

    packed = pl.pallas_call(
        half_pack_kernel,
        out_shape=array(places, 2, 3),
        in_specs=[hbm] * 3,
        out_specs=vmem,
        scratch_shapes=[pltpu.VMEM((3, rows, width), jnp.bfloat16), pltpu.SemaphoreType.DMA((3,))],
        compiler_params=params,
    )(queries, keys, values)
    mine = lax.all_to_all(packed, AXES, 0, 0, axis_index_groups=HALVES, tiled=True)
    first, second = pl.pallas_call(
        half_kv_kernel,
        out_shape=[array(places, 2)] * 2,
        in_specs=[vmem],
        out_specs=[vmem] * 2,
        compiler_params=params,
    )(mine)
    some = [half[p] for half in HALVES for p in SECOND]
    first = lax.ppermute(first, AXES, [(d, d ^ HALF_BIT) for d in range(2 * places)])
    second = lax.ppermute(second, AXES, [(d, d ^ HALF_BIT) for d in some])
    done = pl.pallas_call(
        half_attend_kernel,
        out_shape=array(places, 2),
        in_specs=[smem] + [vmem] * 3,
        out_specs=vmem,
        compiler_params=params,
    )(span_index, mine, first, second)
    back = lax.all_to_all(done, AXES, 0, 0, axis_index_groups=HALVES, tiled=True)
    return pl.pallas_call(
        half_unpack_kernel,
        out_shape=jax.ShapeDtypeStruct((1, rows, width), jnp.bfloat16),
        in_specs=[vmem],
        out_specs=vmem,
        compiler_params=params,
    )(back)


def solution(mesh):
    spec = P("span", "seq", None)
    groups, ranks = mesh.shape["span"], mesh.shape["seq"]
    body = by_half if (groups, ranks) == (2, 16) else functools.partial(shards, groups, groups * ranks)
    return jax.shard_map(body, mesh=mesh, in_specs=(spec, spec, spec, P()), out_specs=spec, check_vma=False)
```

```python
import functools

import jax
import jax.numpy as jnp
from jax import lax
from jax.experimental import pallas as pl
from jax.experimental.pallas import tpu as pltpu
from jax.sharding import PartitionSpec as P

HEADS = 20
AXES = ("span", "seq")


def slot_heads(slots):
    spread = [d for d in range(slots) if d % 2 == 0] + [d for d in range(slots) if d % 2]
    heads = [0] * slots
    for place, d in enumerate(spread):
        heads[d] = place % HEADS
    return heads, spread[:HEADS]


def pack_kernel(heads, q_hbm, k_hbm, v_hbm, out_ref, held, sems):
    copies = [
        pltpu.make_async_copy(src, held.at[pl.ds(i, 1)], sems.at[i])
        for i, src in enumerate((q_hbm, k_hbm, v_hbm))
    ]
    for c in copies:
        c.start()
    size = out_ref.shape[-1]
    for i, c in enumerate(copies):
        c.wait()
        for slot, head in enumerate(heads):
            out_ref[slot, i] = held[i, :, head * size:(head + 1) * size]


def attend_kernel(groups, span_ref, in_ref, out_ref):
    slots, _, rows, size = in_ref.shape
    per = slots // groups
    tokens = per * rows
    scale = size ** -0.5

    def piece(part, group):
        block = in_ref[pl.ds(group * per, per), part].astype(jnp.float32)
        return block.reshape(tokens, size).astype(jnp.bfloat16)

    def one(group, carry):
        mine = span_ref[group]
        source = jnp.int32(0)
        found = jnp.int32(0)
        for p in range(groups):
            hit = (span_ref[p] == mine - 1).astype(jnp.int32)
            source = source + hit * p
            found = found + hit
        has = found > 0
        q = piece(0, group)
        dims = (((1,), (1,)), ((), ()))
        own = lax.dot_general(q, piece(1, group), dims, preferred_element_type=jnp.float32) * scale
        before = lax.dot_general(q, piece(1, source), dims, preferred_element_type=jnp.float32) * scale
        before = jnp.where(has, before, -1e30)
        top = jnp.maximum(jnp.max(own, -1, keepdims=True), jnp.max(before, -1, keepdims=True))
        own_w = jnp.exp(own - top)
        before_w = jnp.where(has, jnp.exp(before - top), 0.0)
        total = jnp.sum(own_w, -1, keepdims=True) + jnp.sum(before_w, -1, keepdims=True)
        acc = jnp.dot(own_w.astype(jnp.bfloat16), piece(2, group), preferred_element_type=jnp.float32)
        acc += jnp.dot(before_w.astype(jnp.bfloat16), piece(2, source), preferred_element_type=jnp.float32)
        result = (acc / total).reshape(per, rows, size).astype(jnp.bfloat16)
        out_ref[pl.ds(group * per, per)] = result
        return carry

    lax.fori_loop(0, groups, one, 0)


def attend_pair_kernel(span_ref, in_ref, out_ref):
    slots, _, rows, size = in_ref.shape
    tokens = slots * rows
    half = tokens // 2

    def piece(part):
        return in_ref[:, part].astype(jnp.float32).reshape(tokens, size).astype(jnp.bfloat16)

    scores = lax.dot_general(
        piece(0), piece(1), (((1,), (1,)), ((), ())), preferred_element_type=jnp.float32
    ) * (size ** -0.5)
    query_group = lax.broadcasted_iota(jnp.int32, (tokens, tokens), 0) // half
    key_group = lax.broadcasted_iota(jnp.int32, (tokens, tokens), 1) // half
    later = jnp.where(span_ref[0] == 1, 0, 1)
    seen = (query_group == key_group) | (query_group == later)
    scores = jnp.where(seen, scores, -1e30)
    weights = jnp.where(seen, jnp.exp(scores - jnp.max(scores, -1, keepdims=True)), 0.0)
    total = jnp.sum(weights, -1, keepdims=True)
    acc = jnp.dot(weights.astype(jnp.bfloat16), piece(2), preferred_element_type=jnp.float32)
    out_ref[...] = (acc / total).reshape(slots, rows, size).astype(jnp.bfloat16)


def unpack_kernel(places, in_ref, out_ref):
    size = in_ref.shape[-1]
    for head, slot in enumerate(places):
        out_ref[0, :, head * size:(head + 1) * size] = in_ref[slot]


def shards(groups, slots, queries, keys, values, span_index):
    rows, width = queries.shape[1:]
    size = width // HEADS
    heads, places = slot_heads(slots)
    vmem = pl.BlockSpec(memory_space=pltpu.VMEM)
    smem = pl.BlockSpec(memory_space=pltpu.SMEM)
    hbm = pl.BlockSpec(memory_space=pltpu.HBM)
    queries, keys, values = [
        pltpu.with_memory_space_constraint(a, pltpu.HBM) for a in (queries, keys, values)
    ]
    params = pltpu.CompilerParams(vmem_limit_bytes=32 * 2**20)
    packed = pl.pallas_call(
        functools.partial(pack_kernel, heads),
        out_shape=jax.ShapeDtypeStruct((slots, 3, rows, size), jnp.bfloat16),
        in_specs=[hbm] * 3,
        out_specs=vmem,
        scratch_shapes=[pltpu.VMEM((3, rows, width), jnp.bfloat16), pltpu.SemaphoreType.DMA((3,))],
        compiler_params=params,
    )(queries, keys, values)
    whole = lax.all_to_all(packed, AXES, 0, 0, tiled=True)
    done = pl.pallas_call(
        attend_pair_kernel if groups == 2 else functools.partial(attend_kernel, groups),
        out_shape=jax.ShapeDtypeStruct((slots, rows, size), jnp.bfloat16),
        in_specs=[smem, vmem],
        out_specs=vmem,
        compiler_params=params,
    )(span_index, whole)
    back = lax.all_to_all(done, AXES, 0, 0, tiled=True)
    return pl.pallas_call(
        functools.partial(unpack_kernel, places),
        out_shape=jax.ShapeDtypeStruct((1, rows, width), jnp.bfloat16),
        in_specs=[vmem],
        out_specs=vmem,
        compiler_params=params,
    )(back)


X_BIT, CORE_BIT = 16, 1
EIGHTS = [[x + 2 * p + c for p in range(8)] for x in (0, X_BIT) for c in (0, CORE_BIT)]
FIRST_HEADS = (0, 2, 5, 7, 10, 12, 15, 17)
OWNERS = [next((p, h - f) for p, f in enumerate(FIRST_HEADS) if f <= h < f + 3) for h in range(HEADS)]


def eight_pack_kernel(q_hbm, k_hbm, v_hbm, out_ref, held, sems):
    copies = [
        pltpu.make_async_copy(src, held.at[pl.ds(i, 1)], sems.at[i])
        for i, src in enumerate((q_hbm, k_hbm, v_hbm))
    ]
    for c in copies:
        c.start()
    places, _, slots, _, size = out_ref.shape
    for i, c in enumerate(copies):
        c.wait()
        for p in range(places):
            for slot in range(slots):
                head = FIRST_HEADS[p] + slot
                out_ref[p, i, slot] = held[i, :, head * size:(head + 1) * size]


def eight_kv_kernel(in_ref, out_ref):
    out_ref[...] = in_ref[:, 1:3]


def eight_attend_kernel(span_ref, in_ref, own_ref, far_ref, far_own_ref, out_ref):
    places, _, slots, rows, size = in_ref.shape
    tokens = places * rows
    has = span_ref[lax.axis_index("span")] == 1
    near = lax.broadcasted_iota(jnp.int32, (tokens, 4 * tokens), 1) < 2 * tokens
    seen = near | has

    def flat(x):
        return x.astype(jnp.float32).reshape(-1, size).astype(jnp.bfloat16)

    for slot in range(slots):
        q = flat(in_ref[:, 0, slot])
        k, v = [
            jnp.concatenate([flat(in_ref[:, i + 1, slot])] + [flat(r[:, i, slot]) for r in (own_ref, far_ref, far_own_ref)], 0)
            for i in range(2)
        ]
        scores = lax.dot_general(
            q, k, (((1,), (1,)), ((), ())), preferred_element_type=jnp.float32
        ) * (size ** -0.5)
        scores = jnp.where(seen, scores, -1e30)
        weights = jnp.where(seen, jnp.exp(scores - jnp.max(scores, -1, keepdims=True)), 0.0)
        total = jnp.sum(weights, -1, keepdims=True)
        acc = jnp.dot(weights.astype(jnp.bfloat16), v, preferred_element_type=jnp.float32)
        out_ref[:, slot] = (acc / total).reshape(places, rows, size).astype(jnp.bfloat16)


def eight_unpack_kernel(in_ref, out_ref):
    size = in_ref.shape[-1]
    for head, (p, slot) in enumerate(OWNERS):
        out_ref[0, :, head * size:(head + 1) * size] = in_ref[p, slot]


def by_eight(queries, keys, values, span_index):
    rows, width = queries.shape[1:]
    size = width // HEADS
    vmem = pl.BlockSpec(memory_space=pltpu.VMEM)
    smem = pl.BlockSpec(memory_space=pltpu.SMEM)
    hbm = pl.BlockSpec(memory_space=pltpu.HBM)
    params = pltpu.CompilerParams(vmem_limit_bytes=32 * 2**20)
    queries, keys, values = [
        pltpu.with_memory_space_constraint(a, pltpu.HBM) for a in (queries, keys, values)
    ]

    def array(*shape):
        return jax.ShapeDtypeStruct(shape + (rows, size), jnp.bfloat16)

    def move(x, offset):
        return lax.ppermute(x, AXES, [(d, d ^ offset) for d in range(32)])

    packed = pl.pallas_call(
        eight_pack_kernel,
        out_shape=array(8, 3, 3),
        in_specs=[hbm] * 3,
        out_specs=vmem,
        scratch_shapes=[pltpu.VMEM((3, rows, width), jnp.bfloat16), pltpu.SemaphoreType.DMA((3,))],
        compiler_params=params,
    )(queries, keys, values)
    mine = lax.all_to_all(packed, AXES, 0, 0, axis_index_groups=EIGHTS, tiled=True)
    kv = pl.pallas_call(
        eight_kv_kernel, out_shape=array(8, 2, 3), in_specs=[vmem], out_specs=vmem, compiler_params=params
    )(mine)
    far = move(kv, X_BIT)
    own = move(kv, CORE_BIT)
    far_own = move(far, CORE_BIT)
    done = pl.pallas_call(
        eight_attend_kernel,
        out_shape=array(8, 3),
        in_specs=[smem] + [vmem] * 4,
        out_specs=vmem,
        compiler_params=params,
    )(span_index, mine, own, far, far_own)
    back = lax.all_to_all(done, AXES, 0, 0, axis_index_groups=EIGHTS, tiled=True)
    return pl.pallas_call(
        eight_unpack_kernel,
        out_shape=jax.ShapeDtypeStruct((1, rows, width), jnp.bfloat16),
        in_specs=[vmem],
        out_specs=vmem,
        compiler_params=params,
    )(back)


def solution(mesh):
    spec = P("span", "seq", None)
    groups, ranks = mesh.shape["span"], mesh.shape["seq"]
    body = by_eight if (groups, ranks) == (2, 16) else functools.partial(shards, groups, groups * ranks)
    return jax.shard_map(body, mesh=mesh, in_specs=(spec, spec, spec, P()), out_specs=spec, check_vma=False)
```

```python
import functools

import jax
import jax.numpy as jnp
from jax import lax
from jax.experimental import pallas as pl
from jax.experimental.pallas import tpu as pltpu
from jax.sharding import PartitionSpec as P

HEADS = 20
AXES = ("span", "seq")


def slot_heads(slots):
    spread = [d for d in range(slots) if d % 2 == 0] + [d for d in range(slots) if d % 2]
    heads = [0] * slots
    for place, d in enumerate(spread):
        heads[d] = place % HEADS
    return heads, spread[:HEADS]


def pack_kernel(heads, q_hbm, k_hbm, v_hbm, out_ref, held, sems):
    copies = [
        pltpu.make_async_copy(src, held.at[pl.ds(i, 1)], sems.at[i])
        for i, src in enumerate((q_hbm, k_hbm, v_hbm))
    ]
    for c in copies:
        c.start()
    size = out_ref.shape[-1]
    for i, c in enumerate(copies):
        c.wait()
        for slot, head in enumerate(heads):
            out_ref[slot, i] = held[i, :, head * size:(head + 1) * size]


def attend_kernel(groups, span_ref, in_ref, out_ref):
    slots, _, rows, size = in_ref.shape
    per = slots // groups
    tokens = per * rows
    scale = size ** -0.5

    def piece(part, group):
        block = in_ref[pl.ds(group * per, per), part].astype(jnp.float32)
        return block.reshape(tokens, size).astype(jnp.bfloat16)

    def one(group, carry):
        mine = span_ref[group]
        source = jnp.int32(0)
        found = jnp.int32(0)
        for p in range(groups):
            hit = (span_ref[p] == mine - 1).astype(jnp.int32)
            source = source + hit * p
            found = found + hit
        has = found > 0
        q = piece(0, group)
        dims = (((1,), (1,)), ((), ()))
        own = lax.dot_general(q, piece(1, group), dims, preferred_element_type=jnp.float32) * scale
        before = lax.dot_general(q, piece(1, source), dims, preferred_element_type=jnp.float32) * scale
        before = jnp.where(has, before, -1e30)
        top = jnp.maximum(jnp.max(own, -1, keepdims=True), jnp.max(before, -1, keepdims=True))
        own_w = jnp.exp(own - top)
        before_w = jnp.where(has, jnp.exp(before - top), 0.0)
        total = jnp.sum(own_w, -1, keepdims=True) + jnp.sum(before_w, -1, keepdims=True)
        acc = jnp.dot(own_w.astype(jnp.bfloat16), piece(2, group), preferred_element_type=jnp.float32)
        acc += jnp.dot(before_w.astype(jnp.bfloat16), piece(2, source), preferred_element_type=jnp.float32)
        result = (acc / total).reshape(per, rows, size).astype(jnp.bfloat16)
        out_ref[pl.ds(group * per, per)] = result
        return carry

    lax.fori_loop(0, groups, one, 0)


def attend_pair_kernel(span_ref, in_ref, out_ref):
    slots, _, rows, size = in_ref.shape
    tokens = slots * rows
    half = tokens // 2

    def piece(part):
        return in_ref[:, part].astype(jnp.float32).reshape(tokens, size).astype(jnp.bfloat16)

    scores = lax.dot_general(
        piece(0), piece(1), (((1,), (1,)), ((), ())), preferred_element_type=jnp.float32
    ) * (size ** -0.5)
    query_group = lax.broadcasted_iota(jnp.int32, (tokens, tokens), 0) // half
    key_group = lax.broadcasted_iota(jnp.int32, (tokens, tokens), 1) // half
    later = jnp.where(span_ref[0] == 1, 0, 1)
    seen = (query_group == key_group) | (query_group == later)
    scores = jnp.where(seen, scores, -1e30)
    weights = jnp.where(seen, jnp.exp(scores - jnp.max(scores, -1, keepdims=True)), 0.0)
    total = jnp.sum(weights, -1, keepdims=True)
    acc = jnp.dot(weights.astype(jnp.bfloat16), piece(2), preferred_element_type=jnp.float32)
    out_ref[...] = (acc / total).reshape(slots, rows, size).astype(jnp.bfloat16)


def unpack_kernel(places, in_ref, out_ref):
    size = in_ref.shape[-1]
    for head, slot in enumerate(places):
        out_ref[0, :, head * size:(head + 1) * size] = in_ref[slot]


def shards(groups, slots, queries, keys, values, span_index):
    rows, width = queries.shape[1:]
    size = width // HEADS
    heads, places = slot_heads(slots)
    vmem = pl.BlockSpec(memory_space=pltpu.VMEM)
    smem = pl.BlockSpec(memory_space=pltpu.SMEM)
    hbm = pl.BlockSpec(memory_space=pltpu.HBM)
    queries, keys, values = [
        pltpu.with_memory_space_constraint(a, pltpu.HBM) for a in (queries, keys, values)
    ]
    params = pltpu.CompilerParams(vmem_limit_bytes=32 * 2**20)
    packed = pl.pallas_call(
        functools.partial(pack_kernel, heads),
        out_shape=jax.ShapeDtypeStruct((slots, 3, rows, size), jnp.bfloat16),
        in_specs=[hbm] * 3,
        out_specs=vmem,
        scratch_shapes=[pltpu.VMEM((3, rows, width), jnp.bfloat16), pltpu.SemaphoreType.DMA((3,))],
        compiler_params=params,
    )(queries, keys, values)
    whole = lax.all_to_all(packed, AXES, 0, 0, tiled=True)
    done = pl.pallas_call(
        attend_pair_kernel if groups == 2 else functools.partial(attend_kernel, groups),
        out_shape=jax.ShapeDtypeStruct((slots, rows, size), jnp.bfloat16),
        in_specs=[smem, vmem],
        out_specs=vmem,
        compiler_params=params,
    )(span_index, whole)
    back = lax.all_to_all(done, AXES, 0, 0, tiled=True)
    return pl.pallas_call(
        functools.partial(unpack_kernel, places),
        out_shape=jax.ShapeDtypeStruct((1, rows, width), jnp.bfloat16),
        in_specs=[vmem],
        out_specs=vmem,
        compiler_params=params,
    )(back)


QUADS = [[x + z + p for x in (0, 16) for z in (0, 4, 8, 12)] for p in range(4)]


def quad_place():
    return lax.axis_index("seq") & 3


def quad_pack_kernel(q_hbm, k_hbm, v_hbm, o0, o1, o2, o3, held, sems):
    copies = [
        pltpu.make_async_copy(src, held.at[pl.ds(i, 1)], sems.at[i])
        for i, src in enumerate((q_hbm, k_hbm, v_hbm))
    ]
    for c in copies:
        c.start()
    for c in copies:
        c.wait()
    width = o0.shape[-1]
    place = quad_place()
    for i, out in enumerate((o0, o1, o2, o3)):
        col = pl.multiple_of((place ^ i) * width, 128)
        out[...] = held[:, :, pl.ds(col, width)]


def quad_join_kernel(p0, p1, p2, p3, out_ref):
    for i, p in enumerate((p0, p1, p2, p3)):
        out_ref[0, :, i] = p[1:3]


def quad_attend_kernel(span_ref, p0, p1, p2, p3, kv_ref, o0, o1, o2, o3):
    rows, width = p0.shape[1:]
    size = width // (HEADS // 4)
    tokens = kv_ref.shape[0] * 4 * rows
    group = lax.axis_index("span")
    has = span_ref[group] == 1
    key_group = lax.broadcasted_iota(jnp.int32, (4 * rows, tokens), 1) // (tokens // 2)
    seen = (key_group == group) | has
    for h in range(width // size):
        cols = slice(h * size, (h + 1) * size)
        q = jnp.concatenate([p[0, :, cols].astype(jnp.float32) for p in (p0, p1, p2, p3)], 0)
        k, v = [
            kv_ref[:, i, :, :, cols].astype(jnp.float32).reshape(tokens, size).astype(jnp.bfloat16)
            for i in range(2)
        ]
        scores = lax.dot_general(
            q.astype(jnp.bfloat16), k, (((1,), (1,)), ((), ())), preferred_element_type=jnp.float32
        ) * (size ** -0.5)
        scores = jnp.where(seen, scores, -1e30)
        weights = jnp.where(seen, jnp.exp(scores - jnp.max(scores, -1, keepdims=True)), 0.0)
        total = jnp.sum(weights, -1, keepdims=True)
        acc = jnp.dot(weights.astype(jnp.bfloat16), v, preferred_element_type=jnp.float32)
        result = acc / total
        for i, out in enumerate((o0, o1, o2, o3)):
            out[:, cols] = result[i * rows:(i + 1) * rows].astype(jnp.bfloat16)


def quad_unpack_kernel(r0, r1, r2, r3, out_ref):
    width = r0.shape[-1]
    place = quad_place()
    for i, r in enumerate((r0, r1, r2, r3)):
        col = pl.multiple_of((place ^ i) * width, 128)
        out_ref[0, :, pl.ds(col, width)] = r[...]


def by_quad(queries, keys, values, span_index):
    rows, full = queries.shape[1:]
    width = full // 4
    vmem = pl.BlockSpec(memory_space=pltpu.VMEM)
    smem = pl.BlockSpec(memory_space=pltpu.SMEM)
    hbm = pl.BlockSpec(memory_space=pltpu.HBM)
    params = pltpu.CompilerParams(vmem_limit_bytes=32 * 2**20)
    queries, keys, values = [
        pltpu.with_memory_space_constraint(a, pltpu.HBM) for a in (queries, keys, values)
    ]

    def array(*shape):
        return jax.ShapeDtypeStruct(shape + (rows, width), jnp.bfloat16)

    def spread(parts):
        return [parts[0]] + [
            lax.ppermute(p, AXES, [(d, d ^ i) for d in range(32)]) for i, p in enumerate(parts) if i
        ]

    parts = pl.pallas_call(
        quad_pack_kernel,
        out_shape=[array(3)] * 4,
        in_specs=[hbm] * 3,
        out_specs=[vmem] * 4,
        scratch_shapes=[pltpu.VMEM((3, rows, full), jnp.bfloat16), pltpu.SemaphoreType.DMA((3,))],
        compiler_params=params,
    )(queries, keys, values)
    parts = spread(parts)
    block = pl.pallas_call(
        quad_join_kernel, out_shape=array(1, 2, 4), in_specs=[vmem] * 4, out_specs=vmem, compiler_params=params
    )(*parts)
    blocks = lax.all_gather(block, AXES, axis=0, axis_index_groups=QUADS, tiled=True)
    done = pl.pallas_call(
        quad_attend_kernel,
        out_shape=[array()] * 4,
        in_specs=[smem] + [vmem] * 5,
        out_specs=[vmem] * 4,
        compiler_params=params,
    )(span_index, *parts, blocks)
    return pl.pallas_call(
        quad_unpack_kernel,
        out_shape=jax.ShapeDtypeStruct((1, rows, full), jnp.bfloat16),
        in_specs=[vmem] * 4,
        out_specs=vmem,
        compiler_params=params,
    )(*spread(done))


def solution(mesh):
    spec = P("span", "seq", None)
    groups, ranks = mesh.shape["span"], mesh.shape["seq"]
    body = by_quad if (groups, ranks) == (2, 16) else functools.partial(shards, groups, groups * ranks)
    return jax.shard_map(body, mesh=mesh, in_specs=(spec, spec, spec, P()), out_specs=spec, check_vma=False)
```

```python
import functools

import jax
import jax.numpy as jnp
from jax import lax
from jax.experimental import pallas as pl
from jax.experimental.pallas import tpu as pltpu
from jax.sharding import PartitionSpec as P

HEADS = 20
AXES = ("span", "seq")


def slot_heads(slots):
    spread = [d for d in range(slots) if d % 2 == 0] + [d for d in range(slots) if d % 2]
    heads = [0] * slots
    for place, d in enumerate(spread):
        heads[d] = place % HEADS
    return heads, spread[:HEADS]


def rank_order(groups, ranks):
    per = [r for c in range(2) for y in range(2) for r in range(ranks) if r % 4 == 2 * y + c]
    return [g * ranks + r for g in range(groups) for r in per]


def pack_kernel(heads, q_hbm, k_hbm, v_hbm, out_ref, held, sems):
    copies = [
        pltpu.make_async_copy(src, held.at[pl.ds(i, 1)], sems.at[i])
        for i, src in enumerate((q_hbm, k_hbm, v_hbm))
    ]
    for c in copies:
        c.start()
    size = out_ref.shape[-1]
    for i, c in enumerate(copies):
        c.wait()
        for slot, head in enumerate(heads):
            out_ref[slot, i] = held[i, :, head * size:(head + 1) * size]


def attend_kernel(groups, span_ref, in_ref, out_ref):
    slots, _, rows, size = in_ref.shape
    per = slots // groups
    tokens = per * rows
    scale = size ** -0.5

    def piece(part, group):
        block = in_ref[pl.ds(group * per, per), part].astype(jnp.float32)
        return block.reshape(tokens, size).astype(jnp.bfloat16)

    def one(group, carry):
        mine = span_ref[group]
        source = jnp.int32(0)
        found = jnp.int32(0)
        for p in range(groups):
            hit = (span_ref[p] == mine - 1).astype(jnp.int32)
            source = source + hit * p
            found = found + hit
        has = found > 0
        q = piece(0, group)
        dims = (((1,), (1,)), ((), ()))
        own = lax.dot_general(q, piece(1, group), dims, preferred_element_type=jnp.float32) * scale
        before = lax.dot_general(q, piece(1, source), dims, preferred_element_type=jnp.float32) * scale
        before = jnp.where(has, before, -1e30)
        top = jnp.maximum(jnp.max(own, -1, keepdims=True), jnp.max(before, -1, keepdims=True))
        own_w = jnp.exp(own - top)
        before_w = jnp.where(has, jnp.exp(before - top), 0.0)
        total = jnp.sum(own_w, -1, keepdims=True) + jnp.sum(before_w, -1, keepdims=True)
        acc = jnp.dot(own_w.astype(jnp.bfloat16), piece(2, group), preferred_element_type=jnp.float32)
        acc += jnp.dot(before_w.astype(jnp.bfloat16), piece(2, source), preferred_element_type=jnp.float32)
        result = (acc / total).reshape(per, rows, size).astype(jnp.bfloat16)
        out_ref[pl.ds(group * per, per)] = result
        return carry

    lax.fori_loop(0, groups, one, 0)


def attend_pair_kernel(span_ref, in_ref, out_ref):
    slots, _, rows, size = in_ref.shape
    tokens = slots * rows
    half = tokens // 2
    later = jnp.where(span_ref[0] == 1, 0, 1)
    key_group = lax.broadcasted_iota(jnp.int32, (half, tokens), 1) // half

    def piece(part, at=slice(None)):
        return in_ref[at, part].astype(jnp.float32).reshape(-1, size).astype(jnp.bfloat16)

    k = piece(1)
    v = jnp.concatenate([piece(2), jnp.ones((tokens, size), jnp.bfloat16)], 1)
    for group in range(2):
        at = slice(group * slots // 2, (group + 1) * slots // 2)
        seen = (key_group == group) | (later == group)
        scores = lax.dot_general(
            piece(0, at), k, (((1,), (1,)), ((), ())), preferred_element_type=jnp.float32
        ) * (size ** -0.5)
        scores = jnp.where(seen, scores, -1e30)
        weights = jnp.where(seen, jnp.exp(scores - jnp.max(scores, -1, keepdims=True)), 0.0)
        acc = jnp.dot(weights.astype(jnp.bfloat16), v, preferred_element_type=jnp.float32)
        result = acc[:, :size] / acc[:, size:]
        out_ref[at] = result.reshape(slots // 2, rows, size).astype(jnp.bfloat16)


def unpack_kernel(places, in_ref, out_ref):
    size = in_ref.shape[-1]
    for head, slot in enumerate(places):
        out_ref[0, :, head * size:(head + 1) * size] = in_ref[slot]


def shards(groups, ranks, queries, keys, values, span_index):
    rows, width = queries.shape[1:]
    size = width // HEADS
    slots = groups * ranks
    heads, places = slot_heads(slots)
    order = [rank_order(groups, ranks)] if ranks % 4 == 0 else None
    vmem = pl.BlockSpec(memory_space=pltpu.VMEM)
    smem = pl.BlockSpec(memory_space=pltpu.SMEM)
    hbm = pl.BlockSpec(memory_space=pltpu.HBM)
    queries, keys, values = [
        pltpu.with_memory_space_constraint(a, pltpu.HBM) for a in (queries, keys, values)
    ]
    params = pltpu.CompilerParams(vmem_limit_bytes=32 * 2**20)
    packed = pl.pallas_call(
        functools.partial(pack_kernel, heads),
        out_shape=jax.ShapeDtypeStruct((slots, 3, rows, size), jnp.bfloat16),
        in_specs=[hbm] * 3,
        out_specs=vmem,
        scratch_shapes=[pltpu.VMEM((3, rows, width), jnp.bfloat16), pltpu.SemaphoreType.DMA((3,))],
        compiler_params=params,
    )(queries, keys, values)
    whole = lax.all_to_all(packed, AXES, 0, 0, axis_index_groups=order, tiled=True)
    done = pl.pallas_call(
        attend_pair_kernel if groups == 2 else functools.partial(attend_kernel, groups),
        out_shape=jax.ShapeDtypeStruct((slots, rows, size), jnp.bfloat16),
        in_specs=[smem, vmem],
        out_specs=vmem,
        compiler_params=params,
    )(span_index, whole)
    back = lax.all_to_all(done, AXES, 0, 0, axis_index_groups=order, tiled=True)
    return pl.pallas_call(
        functools.partial(unpack_kernel, places),
        out_shape=jax.ShapeDtypeStruct((1, rows, width), jnp.bfloat16),
        in_specs=[vmem],
        out_specs=vmem,
        compiler_params=params,
    )(back)


def solution(mesh):
    spec = P("span", "seq", None)
    body = functools.partial(shards, mesh.shape["span"], mesh.shape["seq"])
    return jax.shard_map(body, mesh=mesh, in_specs=(spec, spec, spec, P()), out_specs=spec, check_vma=False)
```

```python
import functools

import jax
import jax.numpy as jnp
from jax import lax
from jax.experimental import pallas as pl
from jax.experimental.pallas import tpu as pltpu
from jax.sharding import PartitionSpec as P

HEADS = 20
AXES = ("span", "seq")


def slot_heads(slots):
    spread = [d for d in range(slots) if d % 2 == 0] + [d for d in range(slots) if d % 2]
    heads = [0] * slots
    for place, d in enumerate(spread):
        heads[d] = place % HEADS
    return heads, spread[:HEADS]


def rank_order(groups, ranks):
    per = [r for c in range(2) for y in range(2) for r in range(ranks) if r % 4 == 2 * y + c]
    return [g * ranks + r for g in range(groups) for r in per]


def pack_kernel(heads, q_hbm, k_hbm, v_hbm, span_hbm, out_ref, flag_ref, held, spans, sems):
    copies = [
        pltpu.make_async_copy(src, held.at[pl.ds(i, 1)], sems.at[i])
        for i, src in enumerate((q_hbm, k_hbm, v_hbm))
    ]
    index = pltpu.make_async_copy(span_hbm, spans, sems.at[3])
    index.start()
    for c in copies:
        c.start()
    size = out_ref.shape[-1]
    for i, c in enumerate(copies):
        c.wait()
        for slot, head in enumerate(heads):
            out_ref[slot, i] = held[i, :, head * size:(head + 1) * size]
    index.wait()
    for group in range(spans.shape[0]):
        flag_ref[group:group + 1] = jnp.full((1, flag_ref.shape[1]), spans[group], jnp.int32)


def attend_kernel(groups, span_ref, in_ref, out_ref):
    slots, _, rows, size = in_ref.shape
    per = slots // groups
    tokens = per * rows
    scale = size ** -0.5

    def piece(part, group):
        block = in_ref[pl.ds(group * per, per), part].astype(jnp.float32)
        return block.reshape(tokens, size).astype(jnp.bfloat16)

    def one(group, carry):
        mine = span_ref[group]
        source = jnp.int32(0)
        found = jnp.int32(0)
        for p in range(groups):
            hit = (span_ref[p] == mine - 1).astype(jnp.int32)
            source = source + hit * p
            found = found + hit
        has = found > 0
        q = piece(0, group)
        dims = (((1,), (1,)), ((), ()))
        own = lax.dot_general(q, piece(1, group), dims, preferred_element_type=jnp.float32) * scale
        before = lax.dot_general(q, piece(1, source), dims, preferred_element_type=jnp.float32) * scale
        before = jnp.where(has, before, -1e30)
        top = jnp.maximum(jnp.max(own, -1, keepdims=True), jnp.max(before, -1, keepdims=True))
        own_w = jnp.exp(own - top)
        before_w = jnp.where(has, jnp.exp(before - top), 0.0)
        total = jnp.sum(own_w, -1, keepdims=True) + jnp.sum(before_w, -1, keepdims=True)
        acc = jnp.dot(own_w.astype(jnp.bfloat16), piece(2, group), preferred_element_type=jnp.float32)
        acc += jnp.dot(before_w.astype(jnp.bfloat16), piece(2, source), preferred_element_type=jnp.float32)
        result = (acc / total).reshape(per, rows, size).astype(jnp.bfloat16)
        out_ref[pl.ds(group * per, per)] = result
        return carry

    lax.fori_loop(0, groups, one, 0)


def attend_pair_kernel(flag_ref, in_ref, out_ref):
    slots, _, rows, size = in_ref.shape
    tokens = slots * rows
    half = tokens // 2
    key_group = lax.broadcasted_iota(jnp.int32, (1, tokens), 1) // half

    def piece(part, at=slice(None)):
        return in_ref[at, part].astype(jnp.float32).reshape(-1, size).astype(jnp.bfloat16)

    k, v = piece(1), piece(2)
    for group in range(2):
        at = slice(group * slots // 2, (group + 1) * slots // 2)
        seen = (key_group == group) | (flag_ref[group:group + 1] == 1)
        scores = lax.dot_general(
            piece(0, at), k, (((1,), (1,)), ((), ())), preferred_element_type=jnp.float32
        ) * (size ** -0.5)
        scores = jnp.where(seen, scores, -1e30)
        weights = jnp.where(seen, jnp.exp(scores - jnp.max(scores, -1, keepdims=True)), 0.0)
        total = jnp.sum(weights, -1, keepdims=True)
        acc = jnp.dot(weights.astype(jnp.bfloat16), v, preferred_element_type=jnp.float32)
        out_ref[at] = (acc / total).reshape(slots // 2, rows, size).astype(jnp.bfloat16)


def unpack_kernel(places, in_ref, out_ref):
    size = in_ref.shape[-1]
    for head, slot in enumerate(places):
        out_ref[0, :, head * size:(head + 1) * size] = in_ref[slot]


def shards(groups, ranks, queries, keys, values, span_index):
    rows, width = queries.shape[1:]
    size = width // HEADS
    slots = groups * ranks
    heads, places = slot_heads(slots)
    order = [rank_order(groups, ranks)] if ranks % 4 == 0 else None
    vmem = pl.BlockSpec(memory_space=pltpu.VMEM)
    smem = pl.BlockSpec(memory_space=pltpu.SMEM)
    hbm = pl.BlockSpec(memory_space=pltpu.HBM)
    queries, keys, values = [
        pltpu.with_memory_space_constraint(a, pltpu.HBM) for a in (queries, keys, values)
    ]
    params = pltpu.CompilerParams(vmem_limit_bytes=32 * 2**20)
    span_index = pltpu.with_memory_space_constraint(span_index, pltpu.HBM)
    packed, flags = pl.pallas_call(
        functools.partial(pack_kernel, heads),
        out_shape=[
            jax.ShapeDtypeStruct((slots, 3, rows, size), jnp.bfloat16),
            jax.ShapeDtypeStruct((groups, slots * rows), jnp.int32),
        ],
        in_specs=[hbm] * 4,
        out_specs=[vmem] * 2,
        scratch_shapes=[
            pltpu.VMEM((3, rows, width), jnp.bfloat16),
            pltpu.SMEM((groups,), jnp.int32),
            pltpu.SemaphoreType.DMA((4,)),
        ],
        compiler_params=params,
    )(queries, keys, values, span_index)
    whole = lax.all_to_all(packed, AXES, 0, 0, axis_index_groups=order, tiled=True)
    pair = groups == 2
    done = pl.pallas_call(
        attend_pair_kernel if pair else functools.partial(attend_kernel, groups),
        out_shape=jax.ShapeDtypeStruct((slots, rows, size), jnp.bfloat16),
        in_specs=[vmem if pair else smem, vmem],
        out_specs=vmem,
        compiler_params=params,
    )(flags if pair else span_index, whole)
    back = lax.all_to_all(done, AXES, 0, 0, axis_index_groups=order, tiled=True)
    return pl.pallas_call(
        functools.partial(unpack_kernel, places),
        out_shape=jax.ShapeDtypeStruct((1, rows, width), jnp.bfloat16),
        in_specs=[vmem],
        out_specs=vmem,
        compiler_params=params,
    )(back)


def solution(mesh):
    spec = P("span", "seq", None)
    body = functools.partial(shards, mesh.shape["span"], mesh.shape["seq"])
    return jax.shard_map(body, mesh=mesh, in_specs=(spec, spec, spec, P()), out_specs=spec, check_vma=False)
```

```python
import functools

import jax
import jax.numpy as jnp
from jax import lax
from jax.experimental import pallas as pl
from jax.experimental.pallas import tpu as pltpu
from jax.sharding import PartitionSpec as P

HEADS = 20
CHUNKS = 4
AXES = ("span", "seq")


def slot_heads(slots):
    spread = [d for d in range(slots) if d % 2 == 0] + [d for d in range(slots) if d % 2]
    heads = [0] * slots
    for place, d in enumerate(spread):
        heads[d] = place % HEADS
    return heads, spread[:HEADS]


def rank_order(groups, ranks):
    per = [r for c in range(2) for y in range(2) for r in range(ranks) if r % 4 == 2 * y + c]
    return [g * ranks + r for g in range(groups) for r in per]


def pack_kernel(heads, q_hbm, k_hbm, v_hbm, span_hbm, out_ref, flag_ref, held, spans, sems, span_sem):
    size = out_ref.shape[-1]
    run = HEADS // CHUNKS
    index = pltpu.make_async_copy(span_hbm, spans, span_sem)
    copies = []
    for i, src in enumerate((q_hbm, k_hbm, v_hbm)):
        for j in range(CHUNKS):
            cols = pl.ds(j * run * size, run * size)
            copies.append(pltpu.make_async_copy(src.at[:, :, cols], held.at[pl.ds(i, 1), :, cols], sems.at[i, j]))
    for c in copies:
        c.start()
    index.start()
    for n, c in enumerate(copies):
        c.wait()
        i, j = n // CHUNKS, n % CHUNKS
        for slot, head in enumerate(heads):
            if head // run == j:
                out_ref[slot, i] = held[i, :, head * size:(head + 1) * size]
    index.wait()
    for group in range(spans.shape[0]):
        flag_ref[group:group + 1] = jnp.full((1, flag_ref.shape[1]), spans[group], jnp.int32)


def attend_kernel(groups, span_ref, in_ref, out_ref):
    slots, _, rows, size = in_ref.shape
    per = slots // groups
    tokens = per * rows
    scale = size ** -0.5

    def piece(part, group):
        block = in_ref[pl.ds(group * per, per), part].astype(jnp.float32)
        return block.reshape(tokens, size).astype(jnp.bfloat16)

    def one(group, carry):
        mine = span_ref[group]
        source = jnp.int32(0)
        found = jnp.int32(0)
        for p in range(groups):
            hit = (span_ref[p] == mine - 1).astype(jnp.int32)
            source = source + hit * p
            found = found + hit
        has = found > 0
        q = piece(0, group)
        dims = (((1,), (1,)), ((), ()))
        own = lax.dot_general(q, piece(1, group), dims, preferred_element_type=jnp.float32) * scale
        before = lax.dot_general(q, piece(1, source), dims, preferred_element_type=jnp.float32) * scale
        before = jnp.where(has, before, -1e30)
        top = jnp.maximum(jnp.max(own, -1, keepdims=True), jnp.max(before, -1, keepdims=True))
        own_w = jnp.exp(own - top)
        before_w = jnp.where(has, jnp.exp(before - top), 0.0)
        total = jnp.sum(own_w, -1, keepdims=True) + jnp.sum(before_w, -1, keepdims=True)
        acc = jnp.dot(own_w.astype(jnp.bfloat16), piece(2, group), preferred_element_type=jnp.float32)
        acc += jnp.dot(before_w.astype(jnp.bfloat16), piece(2, source), preferred_element_type=jnp.float32)
        result = (acc / total).reshape(per, rows, size).astype(jnp.bfloat16)
        out_ref[pl.ds(group * per, per)] = result
        return carry

    lax.fori_loop(0, groups, one, 0)


def attend_pair_kernel(flag_ref, in_ref, out_ref):
    slots, _, rows, size = in_ref.shape
    tokens = slots * rows
    half = tokens // 2
    key_group = lax.broadcasted_iota(jnp.int32, (1, tokens), 1) // half

    def piece(part, at=slice(None)):
        return in_ref[at, part].astype(jnp.float32).reshape(-1, size).astype(jnp.bfloat16)

    k, v = piece(1), piece(2)
    for group in range(2):
        at = slice(group * slots // 2, (group + 1) * slots // 2)
        seen = (key_group == group) | (flag_ref[group:group + 1] == 1)
        scores = lax.dot_general(
            piece(0, at), k, (((1,), (1,)), ((), ())), preferred_element_type=jnp.float32
        ) * (size ** -0.5)
        scores = jnp.where(seen, scores, -1e30)
        weights = jnp.where(seen, jnp.exp(scores - jnp.max(scores, -1, keepdims=True)), 0.0)
        total = jnp.sum(weights, -1, keepdims=True)
        acc = jnp.dot(weights.astype(jnp.bfloat16), v, preferred_element_type=jnp.float32)
        out_ref[at] = (acc / total).reshape(slots // 2, rows, size).astype(jnp.bfloat16)


def unpack_kernel(places, in_ref, out_hbm, held, sems):
    size = in_ref.shape[-1]
    run = HEADS // CHUNKS
    copies = []
    for j in range(CHUNKS):
        for head in range(j * run, (j + 1) * run):
            held[0, :, head * size:(head + 1) * size] = in_ref[places[head]]
        cols = pl.ds(j * run * size, run * size)
        copies.append(pltpu.make_async_copy(held.at[:, :, cols], out_hbm.at[:, :, cols], sems.at[j]))
        copies[-1].start()
    for c in copies:
        c.wait()


def shards(groups, ranks, queries, keys, values, span_index):
    rows, width = queries.shape[1:]
    size = width // HEADS
    slots = groups * ranks
    heads, places = slot_heads(slots)
    order = [rank_order(groups, ranks)] if ranks % 4 == 0 else None
    vmem = pl.BlockSpec(memory_space=pltpu.VMEM)
    smem = pl.BlockSpec(memory_space=pltpu.SMEM)
    hbm = pl.BlockSpec(memory_space=pltpu.HBM)
    queries, keys, values = [
        pltpu.with_memory_space_constraint(a, pltpu.HBM) for a in (queries, keys, values)
    ]
    params = pltpu.CompilerParams(vmem_limit_bytes=32 * 2**20)
    span_index = pltpu.with_memory_space_constraint(span_index, pltpu.HBM)
    packed, flags = pl.pallas_call(
        functools.partial(pack_kernel, heads),
        out_shape=[
            jax.ShapeDtypeStruct((slots, 3, rows, size), jnp.bfloat16),
            jax.ShapeDtypeStruct((groups, slots * rows), jnp.int32),
        ],
        in_specs=[hbm] * 4,
        out_specs=[vmem] * 2,
        scratch_shapes=[
            pltpu.VMEM((3, rows, width), jnp.bfloat16),
            pltpu.SMEM((groups,), jnp.int32),
            pltpu.SemaphoreType.DMA((3, CHUNKS)),
            pltpu.SemaphoreType.DMA(()),
        ],
        compiler_params=params,
    )(queries, keys, values, span_index)
    whole = lax.all_to_all(packed, AXES, 0, 0, axis_index_groups=order, tiled=True)
    pair = groups == 2
    done = pl.pallas_call(
        attend_pair_kernel if pair else functools.partial(attend_kernel, groups),
        out_shape=jax.ShapeDtypeStruct((slots, rows, size), jnp.bfloat16),
        in_specs=[vmem if pair else smem, vmem],
        out_specs=vmem,
        compiler_params=params,
    )(flags if pair else span_index, whole)
    back = lax.all_to_all(done, AXES, 0, 0, axis_index_groups=order, tiled=True)
    return pl.pallas_call(
        functools.partial(unpack_kernel, places),
        out_shape=jax.ShapeDtypeStruct((1, rows, width), jnp.bfloat16),
        in_specs=[vmem],
        out_specs=hbm,
        scratch_shapes=[pltpu.VMEM((1, rows, width), jnp.bfloat16), pltpu.SemaphoreType.DMA((CHUNKS,))],
        compiler_params=params,
    )(back)


def solution(mesh):
    spec = P("span", "seq", None)
    body = functools.partial(shards, mesh.shape["span"], mesh.shape["seq"])
    return jax.shard_map(body, mesh=mesh, in_specs=(spec, spec, spec, P()), out_specs=spec, check_vma=False)
```

```python
import functools
import math

import jax
import jax.numpy as jnp
from jax import lax
from jax.experimental import pallas as pl
from jax.experimental.pallas import tpu as pltpu
from jax.sharding import PartitionSpec as P

HEADS = 20
MASKED = -1e30
AXES = ("span", "seq")


def slot_heads(slots):
    spread = [d for d in range(slots) if d % 2 == 0] + [d for d in range(slots) if d % 2]
    heads = [0] * slots
    for place, d in enumerate(spread):
        heads[d] = place % HEADS
    return heads, spread[:HEADS]


def rank_order(groups, ranks):
    per = [r for c in range(2) for y in range(2) for r in range(ranks) if r % 4 == 2 * y + c]
    return [g * ranks + r for g in range(groups) for r in per]


def pack_kernel(heads, q_hbm, k_hbm, v_hbm, span_hbm, out_ref, bias_ref, held, spans, sems):
    copies = [
        pltpu.make_async_copy(src, held.at[pl.ds(i, 1)], sems.at[i])
        for i, src in enumerate((q_hbm, k_hbm, v_hbm))
    ]
    index = pltpu.make_async_copy(span_hbm, spans, sems.at[3])
    index.start()
    for c in copies:
        c.start()
    size = out_ref.shape[-1]
    for i, c in enumerate(copies):
        c.wait()
        for slot, head in enumerate(heads):
            out_ref[slot, i] = held[i, :, head * size:(head + 1) * size]
    index.wait()
    groups, tokens = bias_ref.shape
    key_group = lax.broadcasted_iota(jnp.int32, (1, tokens), 1) // (tokens // groups)
    for group in range(groups):
        seen = key_group == group
        for p in range(groups):
            seen |= (key_group == p) & (spans[p] == spans[group] - 1)
        bias_ref[group:group + 1] = jnp.where(seen, 0.0, MASKED)


def attend_kernel(groups, span_ref, in_ref, out_ref):
    slots, _, rows, size = in_ref.shape
    per = slots // groups
    tokens = per * rows
    scale = size ** -0.5

    def piece(part, group):
        block = in_ref[pl.ds(group * per, per), part].astype(jnp.float32)
        return block.reshape(tokens, size).astype(jnp.bfloat16)

    def one(group, carry):
        mine = span_ref[group]
        source = jnp.int32(0)
        found = jnp.int32(0)
        for p in range(groups):
            hit = (span_ref[p] == mine - 1).astype(jnp.int32)
            source = source + hit * p
            found = found + hit
        has = found > 0
        q = piece(0, group)
        dims = (((1,), (1,)), ((), ()))
        own = lax.dot_general(q, piece(1, group), dims, preferred_element_type=jnp.float32) * scale
        before = lax.dot_general(q, piece(1, source), dims, preferred_element_type=jnp.float32) * scale
        before = jnp.where(has, before, -1e30)
        top = jnp.maximum(jnp.max(own, -1, keepdims=True), jnp.max(before, -1, keepdims=True))
        own_w = jnp.exp(own - top)
        before_w = jnp.where(has, jnp.exp(before - top), 0.0)
        total = jnp.sum(own_w, -1, keepdims=True) + jnp.sum(before_w, -1, keepdims=True)
        acc = jnp.dot(own_w.astype(jnp.bfloat16), piece(2, group), preferred_element_type=jnp.float32)
        acc += jnp.dot(before_w.astype(jnp.bfloat16), piece(2, source), preferred_element_type=jnp.float32)
        result = (acc / total).reshape(per, rows, size).astype(jnp.bfloat16)
        out_ref[pl.ds(group * per, per)] = result
        return carry

    lax.fori_loop(0, groups, one, 0)


def attend_pair_kernel(bias_ref, in_ref, out_ref):
    slots, _, rows, size = in_ref.shape
    scale = size ** -0.5 * math.log2(math.e)

    def piece(part, at=slice(None)):
        return in_ref[at, part].reshape(-1, size)

    k, v = piece(1), piece(2)
    for group in range(2):
        at = slice(group * slots // 2, (group + 1) * slots // 2)
        scores = lax.dot_general(
            piece(0, at), k, (((1,), (1,)), ((), ())), preferred_element_type=jnp.float32
        )
        scores += bias_ref[group:group + 1]
        weights = jnp.exp2((scores - jnp.max(scores, -1, keepdims=True)) * scale)
        share = 1.0 / jnp.sum(weights, -1, keepdims=True)
        acc = jnp.dot(weights.astype(jnp.bfloat16), v, preferred_element_type=jnp.float32)
        out_ref[at] = (acc * share).reshape(slots // 2, rows, size).astype(jnp.bfloat16)


def unpack_kernel(places, in_ref, out_ref):
    size = in_ref.shape[-1]
    for head, slot in enumerate(places):
        out_ref[0, :, head * size:(head + 1) * size] = in_ref[slot]


def shards(groups, ranks, queries, keys, values, span_index):
    rows, width = queries.shape[1:]
    size = width // HEADS
    slots = groups * ranks
    heads, places = slot_heads(slots)
    order = [rank_order(groups, ranks)] if ranks % 4 == 0 else None
    vmem = pl.BlockSpec(memory_space=pltpu.VMEM)
    smem = pl.BlockSpec(memory_space=pltpu.SMEM)
    hbm = pl.BlockSpec(memory_space=pltpu.HBM)
    queries, keys, values = [
        pltpu.with_memory_space_constraint(a, pltpu.HBM) for a in (queries, keys, values)
    ]
    params = pltpu.CompilerParams(vmem_limit_bytes=32 * 2**20)
    span_index = pltpu.with_memory_space_constraint(span_index, pltpu.HBM)
    packed, bias = pl.pallas_call(
        functools.partial(pack_kernel, heads),
        out_shape=[
            jax.ShapeDtypeStruct((slots, 3, rows, size), jnp.bfloat16),
            jax.ShapeDtypeStruct((groups, slots * rows), jnp.float32),
        ],
        in_specs=[hbm] * 4,
        out_specs=[vmem] * 2,
        scratch_shapes=[
            pltpu.VMEM((3, rows, width), jnp.bfloat16),
            pltpu.SMEM((groups,), jnp.int32),
            pltpu.SemaphoreType.DMA((4,)),
        ],
        compiler_params=params,
    )(queries, keys, values, span_index)
    whole = lax.all_to_all(packed, AXES, 0, 0, axis_index_groups=order, tiled=True)
    pair = groups == 2
    done = pl.pallas_call(
        attend_pair_kernel if pair else functools.partial(attend_kernel, groups),
        out_shape=jax.ShapeDtypeStruct((slots, rows, size), jnp.bfloat16),
        in_specs=[vmem if pair else smem, vmem],
        out_specs=vmem,
        compiler_params=params,
    )(bias if pair else span_index, whole)
    back = lax.all_to_all(done, AXES, 0, 0, axis_index_groups=order, tiled=True)
    return pl.pallas_call(
        functools.partial(unpack_kernel, places),
        out_shape=jax.ShapeDtypeStruct((1, rows, width), jnp.bfloat16),
        in_specs=[vmem],
        out_specs=vmem,
        compiler_params=params,
    )(back)


def solution(mesh):
    spec = P("span", "seq", None)
    body = functools.partial(shards, mesh.shape["span"], mesh.shape["seq"])
    return jax.shard_map(body, mesh=mesh, in_specs=(spec, spec, spec, P()), out_specs=spec, check_vma=False)
```

```python
import functools
import math

import jax
import jax.numpy as jnp
from jax import lax
from jax.experimental import pallas as pl
from jax.experimental.pallas import tpu as pltpu
from jax.sharding import PartitionSpec as P

HEADS = 20
AXES = ("span", "seq")


def slot_heads(slots):
    spread = [d for d in range(slots) if d % 2 == 0] + [d for d in range(slots) if d % 2]
    heads = [0] * slots
    for place, d in enumerate(spread):
        heads[d] = place % HEADS
    return heads, spread[:HEADS]


def rank_order(groups, ranks):
    per = [r for c in range(2) for y in range(2) for r in range(ranks) if r % 4 == 2 * y + c]
    return [g * ranks + r for g in range(groups) for r in per]


def pack_kernel(heads, q_hbm, k_hbm, v_hbm, span_hbm, out_ref, flag_ref, held, spans, sems):
    copies = [
        pltpu.make_async_copy(src, held.at[pl.ds(i, 1)], sems.at[i])
        for i, src in enumerate((q_hbm, k_hbm, v_hbm))
    ]
    index = pltpu.make_async_copy(span_hbm, spans, sems.at[3])
    index.start()
    for c in copies:
        c.start()
    size = out_ref.shape[-1]
    for i, c in enumerate(copies):
        c.wait()
        for slot, head in enumerate(heads):
            out_ref[slot, i] = held[i, :, head * size:(head + 1) * size]
    index.wait()
    for group in range(spans.shape[0]):
        flag_ref[group:group + 1] = jnp.full((1, flag_ref.shape[1]), spans[group], jnp.int32)


def attend_kernel(groups, span_ref, in_ref, out_ref):
    slots, _, rows, size = in_ref.shape
    per = slots // groups
    tokens = per * rows
    scale = size ** -0.5

    def piece(part, group):
        block = in_ref[pl.ds(group * per, per), part].astype(jnp.float32)
        return block.reshape(tokens, size).astype(jnp.bfloat16)

    def one(group, carry):
        mine = span_ref[group]
        source = jnp.int32(0)
        found = jnp.int32(0)
        for p in range(groups):
            hit = (span_ref[p] == mine - 1).astype(jnp.int32)
            source = source + hit * p
            found = found + hit
        has = found > 0
        q = piece(0, group)
        dims = (((1,), (1,)), ((), ()))
        own = lax.dot_general(q, piece(1, group), dims, preferred_element_type=jnp.float32) * scale
        before = lax.dot_general(q, piece(1, source), dims, preferred_element_type=jnp.float32) * scale
        before = jnp.where(has, before, -1e30)
        top = jnp.maximum(jnp.max(own, -1, keepdims=True), jnp.max(before, -1, keepdims=True))
        own_w = jnp.exp(own - top)
        before_w = jnp.where(has, jnp.exp(before - top), 0.0)
        total = jnp.sum(own_w, -1, keepdims=True) + jnp.sum(before_w, -1, keepdims=True)
        acc = jnp.dot(own_w.astype(jnp.bfloat16), piece(2, group), preferred_element_type=jnp.float32)
        acc += jnp.dot(before_w.astype(jnp.bfloat16), piece(2, source), preferred_element_type=jnp.float32)
        result = (acc / total).reshape(per, rows, size).astype(jnp.bfloat16)
        out_ref[pl.ds(group * per, per)] = result
        return carry

    lax.fori_loop(0, groups, one, 0)


def attend_pair_kernel(flag_ref, in_ref, out_ref):
    slots, _, rows, size = in_ref.shape
    tokens = slots * rows
    half = tokens // 2
    key_group = lax.broadcasted_iota(jnp.int32, (1, tokens), 1) // half

    def piece(part, at=slice(None)):
        return in_ref[at, part].astype(jnp.float32).reshape(-1, size).astype(jnp.bfloat16)

    k, v = piece(1), piece(2)
    for group in range(2):
        at = slice(group * slots // 2, (group + 1) * slots // 2)
        seen = (key_group == group) | (flag_ref[group:group + 1] == 1)
        scores = lax.dot_general(
            piece(0, at), k, (((1,), (1,)), ((), ())), preferred_element_type=jnp.float32
        ) * (size ** -0.5)
        scores = jnp.where(seen, scores, -1e30)
        weights = jnp.where(seen, jnp.exp(scores - jnp.max(scores, -1, keepdims=True)), 0.0)
        total = jnp.sum(weights, -1, keepdims=True)
        acc = jnp.dot(weights.astype(jnp.bfloat16), v, preferred_element_type=jnp.float32)
        out_ref[at] = (acc / total).reshape(slots // 2, rows, size).astype(jnp.bfloat16)


def unpack_kernel(places, in_ref, out_ref):
    size = in_ref.shape[-1]
    for head, slot in enumerate(places):
        out_ref[0, :, head * size:(head + 1) * size] = in_ref[slot]


def shards(groups, ranks, queries, keys, values, span_index):
    rows, width = queries.shape[1:]
    size = width // HEADS
    slots = groups * ranks
    heads, places = slot_heads(slots)
    order = [rank_order(groups, ranks)] if ranks % 4 == 0 else None
    vmem = pl.BlockSpec(memory_space=pltpu.VMEM)
    smem = pl.BlockSpec(memory_space=pltpu.SMEM)
    hbm = pl.BlockSpec(memory_space=pltpu.HBM)
    queries, keys, values = [
        pltpu.with_memory_space_constraint(a, pltpu.HBM) for a in (queries, keys, values)
    ]
    params = pltpu.CompilerParams(vmem_limit_bytes=32 * 2**20)
    span_index = pltpu.with_memory_space_constraint(span_index, pltpu.HBM)
    packed, flags = pl.pallas_call(
        functools.partial(pack_kernel, heads),
        out_shape=[
            jax.ShapeDtypeStruct((slots, 3, rows, size), jnp.bfloat16),
            jax.ShapeDtypeStruct((groups, slots * rows), jnp.int32),
        ],
        in_specs=[hbm] * 4,
        out_specs=[vmem] * 2,
        scratch_shapes=[
            pltpu.VMEM((3, rows, width), jnp.bfloat16),
            pltpu.SMEM((groups,), jnp.int32),
            pltpu.SemaphoreType.DMA((4,)),
        ],
        compiler_params=params,
    )(queries, keys, values, span_index)
    whole = lax.all_to_all(packed, AXES, 0, 0, axis_index_groups=order, tiled=True)
    pair = groups == 2
    done = pl.pallas_call(
        attend_pair_kernel if pair else functools.partial(attend_kernel, groups),
        out_shape=jax.ShapeDtypeStruct((slots, rows, size), jnp.bfloat16),
        in_specs=[vmem if pair else smem, vmem],
        out_specs=vmem,
        compiler_params=params,
    )(flags if pair else span_index, whole)
    back = lax.all_to_all(done, AXES, 0, 0, axis_index_groups=order, tiled=True)
    return pl.pallas_call(
        functools.partial(unpack_kernel, places),
        out_shape=jax.ShapeDtypeStruct((1, rows, width), jnp.bfloat16),
        in_specs=[vmem],
        out_specs=vmem,
        compiler_params=params,
    )(back)


LINES = [[x + 4 * z + yc for z in range(4)] for x in (0, 16) for yc in range(4)]


def line_pack_kernel(q_hbm, k_hbm, v_hbm, span_hbm, out_ref, bias_ref, held, spans, sems):
    copies = [
        pltpu.make_async_copy(src, held.at[pl.ds(i, 1)], sems.at[i])
        for i, src in enumerate((q_hbm, k_hbm, v_hbm))
    ]
    index = pltpu.make_async_copy(span_hbm, spans, sems.at[3])
    for c in copies:
        c.start()
    index.start()
    places, _, _, width = out_ref.shape
    for i, c in enumerate(copies):
        c.wait()
        for p in range(places):
            out_ref[p, i] = held[i, :, p * width:(p + 1) * width]
    index.wait()
    bias_ref[...] = jnp.full(bias_ref.shape, jnp.where(spans[lax.axis_index("span")] == 1, 0.0, -1e30))


def line_kv_kernel(in_ref, out_ref):
    out_ref[...] = in_ref[:, 1:3]


def line_attend_kernel(bias_ref, in_ref, *refs):
    blocks, out_ref = refs[:-1], refs[-1]
    places, _, rows, width = in_ref.shape
    size = width * places // HEADS
    scale = size ** -0.5 * math.log2(math.e)
    for h in range(width // size):
        cols = slice(h * size, (h + 1) * size)

        def piece(ref, part):
            return ref[:, part, :, cols].reshape(-1, size)

        q = piece(in_ref, 0)
        k = jnp.concatenate([piece(b, 0) for b in blocks], 0)
        v = jnp.concatenate([piece(b, 1) for b in blocks], 0)
        scores = lax.dot_general(q, k, (((1,), (1,)), ((), ())), preferred_element_type=jnp.float32)
        half = scores.shape[1] // 2
        scores = jnp.concatenate([scores[:, :half], scores[:, half:] + bias_ref[...]], 1)
        weights = jnp.exp2((scores - jnp.max(scores, -1, keepdims=True)) * scale)
        share = 1.0 / jnp.sum(weights, -1, keepdims=True)
        acc = jnp.dot(weights.astype(jnp.bfloat16), v, preferred_element_type=jnp.float32)
        out_ref[:, :, cols] = (acc * share).reshape(places, rows, size).astype(jnp.bfloat16)


def by_line(queries, keys, values, span_index):
    rows, full = queries.shape[1:]
    places = len(LINES[0])
    width = full // places
    vmem = pl.BlockSpec(memory_space=pltpu.VMEM)
    hbm = pl.BlockSpec(memory_space=pltpu.HBM)
    params = pltpu.CompilerParams(vmem_limit_bytes=32 * 2**20)
    args = [pltpu.with_memory_space_constraint(a, pltpu.HBM) for a in (queries, keys, values, span_index)]

    def array(*shape):
        return jax.ShapeDtypeStruct(shape + (rows, width), jnp.bfloat16)

    def move(x, offset):
        return lax.ppermute(x, AXES, [(d, d ^ offset) for d in range(32)])

    packed, bias = pl.pallas_call(
        line_pack_kernel,
        out_shape=[array(places, 3), jax.ShapeDtypeStruct((1, 128), jnp.float32)],
        in_specs=[hbm] * 4,
        out_specs=[vmem] * 2,
        scratch_shapes=[
            pltpu.VMEM((3, rows, full), jnp.bfloat16),
            pltpu.SMEM((2,), jnp.int32),
            pltpu.SemaphoreType.DMA((4,)),
        ],
        compiler_params=params,
    )(*args)
    mine = lax.all_to_all(packed, AXES, 0, 0, axis_index_groups=LINES, tiled=True)
    kv = pl.pallas_call(
        line_kv_kernel, out_shape=array(places, 2), in_specs=[vmem], out_specs=vmem, compiler_params=params
    )(mine)
    x, y, xy = [move(kv, offset) for offset in (16, 2, 18)]
    near, near_y, far, far_y = [move(b, 1) for b in (kv, y, x, xy)]
    done = pl.pallas_call(
        line_attend_kernel,
        out_shape=array(places),
        in_specs=[vmem] * 10,
        out_specs=vmem,
        compiler_params=params,
    )(bias, mine, kv, y, near, near_y, x, xy, far, far_y)
    back = lax.all_to_all(done, AXES, 0, 0, axis_index_groups=LINES, tiled=True)
    return back.transpose(1, 0, 2).reshape(1, rows, full)


def solution(mesh):
    spec = P("span", "seq", None)
    groups, ranks = mesh.shape["span"], mesh.shape["seq"]
    body = by_line if (groups, ranks) == (2, 16) else functools.partial(shards, groups, ranks)
    return jax.shard_map(body, mesh=mesh, in_specs=(spec, spec, spec, P()), out_specs=spec, check_vma=False)
```

```python
import functools
import math

import jax
import jax.numpy as jnp
from jax import lax
from jax.experimental import pallas as pl
from jax.experimental.pallas import tpu as pltpu
from jax.sharding import PartitionSpec as P

HEADS = 20
AXES = ("span", "seq")


def slot_heads(slots):
    spread = [d for d in range(slots) if d % 2 == 0] + [d for d in range(slots) if d % 2]
    heads = [0] * slots
    for place, d in enumerate(spread):
        heads[d] = place % HEADS
    return heads, spread[:HEADS]


def rank_order(groups, ranks):
    per = [r for c in range(2) for y in range(2) for r in range(ranks) if r % 4 == 2 * y + c]
    return [g * ranks + r for g in range(groups) for r in per]


def pack_kernel(heads, q_hbm, k_hbm, v_hbm, span_hbm, out_ref, flag_ref, held, spans, sems):
    copies = [
        pltpu.make_async_copy(src, held.at[pl.ds(i, 1)], sems.at[i])
        for i, src in enumerate((q_hbm, k_hbm, v_hbm))
    ]
    index = pltpu.make_async_copy(span_hbm, spans, sems.at[3])
    index.start()
    for c in copies:
        c.start()
    size = out_ref.shape[-1]
    for i, c in enumerate(copies):
        c.wait()
        for slot, head in enumerate(heads):
            out_ref[slot, i] = held[i, :, head * size:(head + 1) * size]
    index.wait()
    for group in range(spans.shape[0]):
        flag_ref[group:group + 1] = jnp.full((1, flag_ref.shape[1]), spans[group], jnp.int32)


def attend_kernel(groups, span_ref, in_ref, out_ref):
    slots, _, rows, size = in_ref.shape
    per = slots // groups
    tokens = per * rows
    scale = size ** -0.5

    def piece(part, group):
        block = in_ref[pl.ds(group * per, per), part].astype(jnp.float32)
        return block.reshape(tokens, size).astype(jnp.bfloat16)

    def one(group, carry):
        mine = span_ref[group]
        source = jnp.int32(0)
        found = jnp.int32(0)
        for p in range(groups):
            hit = (span_ref[p] == mine - 1).astype(jnp.int32)
            source = source + hit * p
            found = found + hit
        has = found > 0
        q = piece(0, group)
        dims = (((1,), (1,)), ((), ()))
        own = lax.dot_general(q, piece(1, group), dims, preferred_element_type=jnp.float32) * scale
        before = lax.dot_general(q, piece(1, source), dims, preferred_element_type=jnp.float32) * scale
        before = jnp.where(has, before, -1e30)
        top = jnp.maximum(jnp.max(own, -1, keepdims=True), jnp.max(before, -1, keepdims=True))
        own_w = jnp.exp(own - top)
        before_w = jnp.where(has, jnp.exp(before - top), 0.0)
        total = jnp.sum(own_w, -1, keepdims=True) + jnp.sum(before_w, -1, keepdims=True)
        acc = jnp.dot(own_w.astype(jnp.bfloat16), piece(2, group), preferred_element_type=jnp.float32)
        acc += jnp.dot(before_w.astype(jnp.bfloat16), piece(2, source), preferred_element_type=jnp.float32)
        result = (acc / total).reshape(per, rows, size).astype(jnp.bfloat16)
        out_ref[pl.ds(group * per, per)] = result
        return carry

    lax.fori_loop(0, groups, one, 0)


def attend_pair_kernel(flag_ref, in_ref, out_ref):
    slots, _, rows, size = in_ref.shape
    per = slots // 2
    scale = size ** -0.5 * math.log2(math.e)

    def piece(part, at=slice(None)):
        return in_ref[at, part].reshape(-1, size)

    def over(axes, x, y):
        return lax.dot_general(x, y, ((axes, axes), ((), ())), preferred_element_type=jnp.float32)

    for group in range(2):
        at = slice(group * per, (group + 1) * per)
        other = slice((1 - group) * per, (2 - group) * per)
        q = piece(0, at)
        own = over((1,), piece(1, at), q)
        bias = jnp.where(flag_ref[group:group + 1, :own.shape[1]] == 1, 0.0, -1e30)
        before = over((1,), piece(1, other), q) + bias
        top = jnp.max(jnp.maximum(own, before), 0, keepdims=True)
        own_w = jnp.exp2((own - top) * scale)
        before_w = jnp.exp2((before - top) * scale)
        share = 1.0 / jnp.sum(own_w + before_w, 0, keepdims=True)
        acc = over((0,), piece(2, at), own_w.astype(jnp.bfloat16))
        acc += over((0,), piece(2, other), before_w.astype(jnp.bfloat16))
        out_ref[at] = (acc * share).T.reshape(per, rows, size).astype(jnp.bfloat16)


def unpack_kernel(places, in_ref, out_ref):
    size = in_ref.shape[-1]
    for head, slot in enumerate(places):
        out_ref[0, :, head * size:(head + 1) * size] = in_ref[slot]


def shards(groups, ranks, queries, keys, values, span_index):
    rows, width = queries.shape[1:]
    size = width // HEADS
    slots = groups * ranks
    heads, places = slot_heads(slots)
    order = [rank_order(groups, ranks)] if ranks % 4 == 0 else None
    vmem = pl.BlockSpec(memory_space=pltpu.VMEM)
    smem = pl.BlockSpec(memory_space=pltpu.SMEM)
    hbm = pl.BlockSpec(memory_space=pltpu.HBM)
    queries, keys, values = [
        pltpu.with_memory_space_constraint(a, pltpu.HBM) for a in (queries, keys, values)
    ]
    params = pltpu.CompilerParams(vmem_limit_bytes=32 * 2**20)
    span_index = pltpu.with_memory_space_constraint(span_index, pltpu.HBM)
    packed, flags = pl.pallas_call(
        functools.partial(pack_kernel, heads),
        out_shape=[
            jax.ShapeDtypeStruct((slots, 3, rows, size), jnp.bfloat16),
            jax.ShapeDtypeStruct((groups, slots * rows), jnp.int32),
        ],
        in_specs=[hbm] * 4,
        out_specs=[vmem] * 2,
        scratch_shapes=[
            pltpu.VMEM((3, rows, width), jnp.bfloat16),
            pltpu.SMEM((groups,), jnp.int32),
            pltpu.SemaphoreType.DMA((4,)),
        ],
        compiler_params=params,
    )(queries, keys, values, span_index)
    whole = lax.all_to_all(packed, AXES, 0, 0, axis_index_groups=order, tiled=True)
    pair = groups == 2
    done = pl.pallas_call(
        attend_pair_kernel if pair else functools.partial(attend_kernel, groups),
        out_shape=jax.ShapeDtypeStruct((slots, rows, size), jnp.bfloat16),
        in_specs=[vmem if pair else smem, vmem],
        out_specs=vmem,
        compiler_params=params,
    )(flags if pair else span_index, whole)
    back = lax.all_to_all(done, AXES, 0, 0, axis_index_groups=order, tiled=True)
    return pl.pallas_call(
        functools.partial(unpack_kernel, places),
        out_shape=jax.ShapeDtypeStruct((1, rows, width), jnp.bfloat16),
        in_specs=[vmem],
        out_specs=vmem,
        compiler_params=params,
    )(back)


def solution(mesh):
    spec = P("span", "seq", None)
    body = functools.partial(shards, mesh.shape["span"], mesh.shape["seq"])
    return jax.shard_map(body, mesh=mesh, in_specs=(spec, spec, spec, P()), out_specs=spec, check_vma=False)
```

```python
import functools

import jax
import jax.numpy as jnp
from jax import lax
from jax.experimental import pallas as pl
from jax.experimental.pallas import tpu as pltpu
from jax.sharding import PartitionSpec as P

HEADS = 20
AXES = ("span", "seq")


def slot_heads(slots):
    spread = [d for d in range(slots) if d % 2 == 0] + [d for d in range(slots) if d % 2]
    heads = [0] * slots
    for place, d in enumerate(spread):
        heads[d] = place % HEADS
    return heads, spread[:HEADS]


def pack_kernel(heads, q_hbm, k_hbm, v_hbm, span_hbm, out_ref, flag_ref, held, spans, sems):
    copies = [
        pltpu.make_async_copy(src, held.at[pl.ds(i, 1)], sems.at[i])
        for i, src in enumerate((q_hbm, k_hbm, v_hbm))
    ]
    index = pltpu.make_async_copy(span_hbm, spans, sems.at[3])
    index.start()
    for c in copies:
        c.start()
    size = out_ref.shape[-1]
    for i, c in enumerate(copies):
        c.wait()
        for slot, head in enumerate(heads):
            out_ref[slot, i] = held[i, :, head * size:(head + 1) * size]
    index.wait()
    for group in range(spans.shape[0]):
        flag_ref[group:group + 1] = jnp.full((1, flag_ref.shape[1]), spans[group], jnp.int32)


def attend_kernel(groups, span_ref, in_ref, out_ref):
    slots, _, rows, size = in_ref.shape
    per = slots // groups
    tokens = per * rows
    scale = size ** -0.5

    def piece(part, group):
        block = in_ref[pl.ds(group * per, per), part].astype(jnp.float32)
        return block.reshape(tokens, size).astype(jnp.bfloat16)

    def one(group, carry):
        mine = span_ref[group]
        source = jnp.int32(0)
        found = jnp.int32(0)
        for p in range(groups):
            hit = (span_ref[p] == mine - 1).astype(jnp.int32)
            source = source + hit * p
            found = found + hit
        has = found > 0
        q = piece(0, group)
        dims = (((1,), (1,)), ((), ()))
        own = lax.dot_general(q, piece(1, group), dims, preferred_element_type=jnp.float32) * scale
        before = lax.dot_general(q, piece(1, source), dims, preferred_element_type=jnp.float32) * scale
        before = jnp.where(has, before, -1e30)
        top = jnp.maximum(jnp.max(own, -1, keepdims=True), jnp.max(before, -1, keepdims=True))
        own_w = jnp.exp(own - top)
        before_w = jnp.where(has, jnp.exp(before - top), 0.0)
        total = jnp.sum(own_w, -1, keepdims=True) + jnp.sum(before_w, -1, keepdims=True)
        acc = jnp.dot(own_w.astype(jnp.bfloat16), piece(2, group), preferred_element_type=jnp.float32)
        acc += jnp.dot(before_w.astype(jnp.bfloat16), piece(2, source), preferred_element_type=jnp.float32)
        result = (acc / total).reshape(per, rows, size).astype(jnp.bfloat16)
        out_ref[pl.ds(group * per, per)] = result
        return carry

    lax.fori_loop(0, groups, one, 0)


def attend_pair_kernel(flag_ref, in_ref, out_ref):
    slots, _, rows, size = in_ref.shape
    tokens = slots * rows
    run = slots // 4
    key_group = lax.broadcasted_iota(jnp.int32, (1, tokens), 1) // (tokens // 2)

    def piece(part, at=slice(None)):
        return in_ref[at, part].reshape(-1, size)

    k, v = piece(1), piece(2)
    for chain in range(4):
        group = chain // 2
        at = slice(chain * run, (chain + 1) * run)
        seen = (key_group == group) | (flag_ref[group:group + 1] == 1)
        scores = lax.dot_general(
            piece(0, at), k, (((1,), (1,)), ((), ())), preferred_element_type=jnp.float32
        ) * (size ** -0.5)
        scores = jnp.where(seen, scores, -1e30)
        weights = jnp.where(seen, jnp.exp(scores - jnp.max(scores, -1, keepdims=True)), 0.0)
        total = jnp.sum(weights, -1, keepdims=True)
        acc = jnp.dot(weights.astype(jnp.bfloat16), v, preferred_element_type=jnp.float32)
        out_ref[at] = (acc / total).reshape(run, rows, size).astype(jnp.bfloat16)


def unpack_kernel(places, in_ref, out_ref):
    size = in_ref.shape[-1]
    for head, slot in enumerate(places):
        out_ref[0, :, head * size:(head + 1) * size] = in_ref[slot]


def shards(groups, ranks, queries, keys, values, span_index):
    rows, width = queries.shape[1:]
    size = width // HEADS
    slots = groups * ranks
    heads, places = slot_heads(slots)
    vmem = pl.BlockSpec(memory_space=pltpu.VMEM)
    smem = pl.BlockSpec(memory_space=pltpu.SMEM)
    hbm = pl.BlockSpec(memory_space=pltpu.HBM)
    queries, keys, values = [
        pltpu.with_memory_space_constraint(a, pltpu.HBM) for a in (queries, keys, values)
    ]
    params = pltpu.CompilerParams(vmem_limit_bytes=32 * 2**20)
    span_index = pltpu.with_memory_space_constraint(span_index, pltpu.HBM)
    packed, flags = pl.pallas_call(
        functools.partial(pack_kernel, heads),
        out_shape=[
            jax.ShapeDtypeStruct((slots, 3, rows, size), jnp.bfloat16),
            jax.ShapeDtypeStruct((groups, slots * rows), jnp.int32),
        ],
        in_specs=[hbm] * 4,
        out_specs=[vmem] * 2,
        scratch_shapes=[
            pltpu.VMEM((3, rows, width), jnp.bfloat16),
            pltpu.SMEM((groups,), jnp.int32),
            pltpu.SemaphoreType.DMA((4,)),
        ],
        compiler_params=params,
    )(queries, keys, values, span_index)
    whole = lax.all_to_all(packed, AXES, 0, 0, tiled=True)
    pair = groups == 2
    done = pl.pallas_call(
        attend_pair_kernel if pair else functools.partial(attend_kernel, groups),
        out_shape=jax.ShapeDtypeStruct((slots, rows, size), jnp.bfloat16),
        in_specs=[vmem if pair else smem, vmem],
        out_specs=vmem,
        compiler_params=params,
    )(flags if pair else span_index, whole)
    back = lax.all_to_all(done, AXES, 0, 0, tiled=True)
    return pl.pallas_call(
        functools.partial(unpack_kernel, places),
        out_shape=jax.ShapeDtypeStruct((1, rows, width), jnp.bfloat16),
        in_specs=[vmem],
        out_specs=vmem,
        compiler_params=params,
    )(back)


def solution(mesh):
    spec = P("span", "seq", None)
    body = functools.partial(shards, mesh.shape["span"], mesh.shape["seq"])
    return jax.shard_map(body, mesh=mesh, in_specs=(spec, spec, spec, P()), out_specs=spec, check_vma=False)
```

```python
import functools
import math

import jax
import jax.numpy as jnp
from jax import lax
from jax.experimental import pallas as pl
from jax.experimental.pallas import tpu as pltpu
from jax.sharding import PartitionSpec as P

HEADS = 20
MASKED = -1e30
AXES = ("span", "seq")


def slot_heads(slots):
    spread = [d for d in range(slots) if d % 2 == 0] + [d for d in range(slots) if d % 2]
    heads = [0] * slots
    for place, d in enumerate(spread):
        heads[d] = place % HEADS
    return heads, spread[:HEADS]


def way_back(groups, ranks):
    if groups != 2:
        return list(range(groups * ranks))
    per = [r for c in range(2) for y in range(2) for r in range(ranks) if r % 4 == 2 * y + c]
    return [g * ranks + r for g in range(groups) for r in per][::-1]


def pack_kernel(heads, q_hbm, k_hbm, v_hbm, span_hbm, out_ref, bias_ref, held, spans, sems):
    copies = [
        pltpu.make_async_copy(src, held.at[pl.ds(i, 1)], sems.at[i])
        for i, src in enumerate((q_hbm, k_hbm, v_hbm))
    ]
    index = pltpu.make_async_copy(span_hbm, spans, sems.at[3])
    index.start()
    for c in copies:
        c.start()
    size = out_ref.shape[-1]
    for i, c in enumerate(copies):
        c.wait()
        for slot, head in enumerate(heads):
            out_ref[slot, i] = held[i, :, head * size:(head + 1) * size]
    index.wait()
    groups, tokens = bias_ref.shape
    key_group = lax.broadcasted_iota(jnp.int32, (1, tokens), 1) // (tokens // groups)
    for group in range(groups):
        seen = key_group == group
        for p in range(groups):
            seen |= (key_group == p) & (spans[p] == spans[group] - 1)
        bias_ref[group:group + 1] = jnp.where(seen, 0.0, MASKED)


def attend_kernel(order, groups, span_ref, in_ref, out_ref):
    slots, _, rows, size = in_ref.shape
    per = slots // groups
    tokens = per * rows
    scale = size ** -0.5

    def piece(part, group):
        block = in_ref[pl.ds(group * per, per), part].astype(jnp.float32)
        return block.reshape(tokens, size).astype(jnp.bfloat16)

    def one(group, carry):
        mine = span_ref[group]
        source = jnp.int32(0)
        found = jnp.int32(0)
        for p in range(groups):
            hit = (span_ref[p] == mine - 1).astype(jnp.int32)
            source = source + hit * p
            found = found + hit
        has = found > 0
        q = piece(0, group)
        dims = (((1,), (1,)), ((), ()))
        own = lax.dot_general(q, piece(1, group), dims, preferred_element_type=jnp.float32) * scale
        before = lax.dot_general(q, piece(1, source), dims, preferred_element_type=jnp.float32) * scale
        before = jnp.where(has, before, -1e30)
        top = jnp.maximum(jnp.max(own, -1, keepdims=True), jnp.max(before, -1, keepdims=True))
        own_w = jnp.exp(own - top)
        before_w = jnp.where(has, jnp.exp(before - top), 0.0)
        total = jnp.sum(own_w, -1, keepdims=True) + jnp.sum(before_w, -1, keepdims=True)
        acc = jnp.dot(own_w.astype(jnp.bfloat16), piece(2, group), preferred_element_type=jnp.float32)
        acc += jnp.dot(before_w.astype(jnp.bfloat16), piece(2, source), preferred_element_type=jnp.float32)
        result = (acc / total).reshape(per, rows, size).astype(jnp.bfloat16)
        out_ref[pl.ds(group * per, per)] = result
        return carry

    lax.fori_loop(0, groups, one, 0)


def attend_pair_kernel(order, groups, bias_ref, in_ref, out_ref):
    slots, _, rows, size = in_ref.shape
    half = slots * rows // 2

    def piece(part):
        return in_ref[:, part].reshape(-1, size)

    scores = lax.dot_general(
        piece(0), piece(1), (((1,), (1,)), ((), ())), preferred_element_type=jnp.float32
    )
    scores = jnp.concatenate([scores[:half] + bias_ref[0:1], scores[half:] + bias_ref[1:2]], 0)
    scale = size ** -0.5 * math.log2(math.e)
    weights = jnp.exp2((scores - jnp.max(scores, -1, keepdims=True)) * scale)
    share = 1.0 / jnp.sum(weights, -1, keepdims=True)
    acc = jnp.dot(weights.astype(jnp.bfloat16), piece(2), preferred_element_type=jnp.float32)
    result = (acc * share).reshape(slots, rows, size)
    for slot, device in enumerate(order):
        out_ref[slot] = result[device].astype(jnp.bfloat16)


def unpack_kernel(places, in_ref, out_ref):
    size = in_ref.shape[-1]
    for head, slot in enumerate(places):
        out_ref[0, :, head * size:(head + 1) * size] = in_ref[slot]


def shards(groups, ranks, queries, keys, values, span_index):
    rows, width = queries.shape[1:]
    size = width // HEADS
    slots = groups * ranks
    heads, places = slot_heads(slots)
    order = way_back(groups, ranks)
    vmem = pl.BlockSpec(memory_space=pltpu.VMEM)
    smem = pl.BlockSpec(memory_space=pltpu.SMEM)
    hbm = pl.BlockSpec(memory_space=pltpu.HBM)
    queries, keys, values = [
        pltpu.with_memory_space_constraint(a, pltpu.HBM) for a in (queries, keys, values)
    ]
    params = pltpu.CompilerParams(vmem_limit_bytes=32 * 2**20)
    span_index = pltpu.with_memory_space_constraint(span_index, pltpu.HBM)
    packed, bias = pl.pallas_call(
        functools.partial(pack_kernel, heads),
        out_shape=[
            jax.ShapeDtypeStruct((slots, 3, rows, size), jnp.bfloat16),
            jax.ShapeDtypeStruct((groups, slots * rows), jnp.float32),
        ],
        in_specs=[hbm] * 4,
        out_specs=[vmem] * 2,
        scratch_shapes=[
            pltpu.VMEM((3, rows, width), jnp.bfloat16),
            pltpu.SMEM((groups,), jnp.int32),
            pltpu.SemaphoreType.DMA((4,)),
        ],
        compiler_params=params,
    )(queries, keys, values, span_index)
    whole = lax.all_to_all(packed, AXES, 0, 0, tiled=True)
    pair = groups == 2
    done = pl.pallas_call(
        functools.partial(attend_pair_kernel if pair else attend_kernel, order, groups),
        out_shape=jax.ShapeDtypeStruct((slots, rows, size), jnp.bfloat16),
        in_specs=[vmem if pair else smem, vmem],
        out_specs=vmem,
        compiler_params=params,
    )(bias if pair else span_index, whole)
    back = lax.all_to_all(done, AXES, 0, 0, axis_index_groups=[order], tiled=True)
    return pl.pallas_call(
        functools.partial(unpack_kernel, [order.index(p) for p in places]),
        out_shape=jax.ShapeDtypeStruct((1, rows, width), jnp.bfloat16),
        in_specs=[vmem],
        out_specs=vmem,
        compiler_params=params,
    )(back)


def solution(mesh):
    spec = P("span", "seq", None)
    body = functools.partial(shards, mesh.shape["span"], mesh.shape["seq"])
    return jax.shard_map(body, mesh=mesh, in_specs=(spec, spec, spec, P()), out_specs=spec, check_vma=False)
```

```python
import functools
import math

import jax
import jax.numpy as jnp
from jax import lax
from jax.experimental import pallas as pl
from jax.experimental.pallas import tpu as pltpu
from jax.sharding import PartitionSpec as P

HEADS = 20
MASKED = -1e30
AXES = ("span", "seq")


def slot_heads(slots):
    spread = [d for d in range(slots) if d % 2 == 0] + [d for d in range(slots) if d % 2]
    heads = [0] * slots
    for place, d in enumerate(spread):
        heads[d] = place % HEADS
    return heads, spread[:HEADS]


def way_back(groups, ranks):
    if groups != 2:
        return list(range(groups * ranks))
    per = [r for c in range(2) for y in range(2) for r in range(ranks) if r % 4 == 2 * y + c]
    return [g * ranks + r for g in range(groups) for r in per]


def pack_kernel(heads, q_hbm, k_hbm, v_hbm, span_hbm, out_ref, bias_ref, held, spans, sems):
    copies = [
        pltpu.make_async_copy(src, held.at[pl.ds(i, 1)], sems.at[i])
        for i, src in enumerate((q_hbm, k_hbm, v_hbm))
    ]
    index = pltpu.make_async_copy(span_hbm, spans, sems.at[3])
    index.start()
    for c in copies:
        c.start()
    size = out_ref.shape[-1]
    for i, c in enumerate(copies):
        c.wait()
        for slot, head in enumerate(heads):
            out_ref[slot, i] = held[i, :, head * size:(head + 1) * size]
    index.wait()
    groups, tokens = bias_ref.shape
    key_group = lax.broadcasted_iota(jnp.int32, (1, tokens), 1) // (tokens // groups)
    for group in range(groups):
        seen = key_group == group
        for p in range(groups):
            seen |= (key_group == p) & (spans[p] == spans[group] - 1)
        bias_ref[group:group + 1] = jnp.where(seen, 0.0, MASKED)


def attend_kernel(order, groups, span_ref, in_ref, out_ref):
    slots, _, rows, size = in_ref.shape
    per = slots // groups
    tokens = per * rows
    scale = size ** -0.5

    def piece(part, group):
        block = in_ref[pl.ds(group * per, per), part].astype(jnp.float32)
        return block.reshape(tokens, size).astype(jnp.bfloat16)

    def one(group, carry):
        mine = span_ref[group]
        source = jnp.int32(0)
        found = jnp.int32(0)
        for p in range(groups):
            hit = (span_ref[p] == mine - 1).astype(jnp.int32)
            source = source + hit * p
            found = found + hit
        has = found > 0
        q = piece(0, group)
        dims = (((1,), (1,)), ((), ()))
        own = lax.dot_general(q, piece(1, group), dims, preferred_element_type=jnp.float32) * scale
        before = lax.dot_general(q, piece(1, source), dims, preferred_element_type=jnp.float32) * scale
        before = jnp.where(has, before, -1e30)
        top = jnp.maximum(jnp.max(own, -1, keepdims=True), jnp.max(before, -1, keepdims=True))
        own_w = jnp.exp(own - top)
        before_w = jnp.where(has, jnp.exp(before - top), 0.0)
        total = jnp.sum(own_w, -1, keepdims=True) + jnp.sum(before_w, -1, keepdims=True)
        acc = jnp.dot(own_w.astype(jnp.bfloat16), piece(2, group), preferred_element_type=jnp.float32)
        acc += jnp.dot(before_w.astype(jnp.bfloat16), piece(2, source), preferred_element_type=jnp.float32)
        result = (acc / total).reshape(per, rows, size).astype(jnp.bfloat16)
        out_ref[pl.ds(group * per, per)] = result
        return carry

    lax.fori_loop(0, groups, one, 0)


def attend_pair_kernel(order, groups, bias_ref, in_ref, out_ref):
    slots, _, rows, size = in_ref.shape
    half = slots * rows // 2

    def piece(part):
        return in_ref[:, part].reshape(-1, size)

    scores = lax.dot_general(
        piece(0), piece(1), (((1,), (1,)), ((), ())), preferred_element_type=jnp.float32
    )
    scores = jnp.concatenate([scores[:half] + bias_ref[0:1], scores[half:] + bias_ref[1:2]], 0)
    scale = size ** -0.5 * math.log2(math.e)
    weights = jnp.exp2((scores - jnp.max(scores, -1, keepdims=True)) * scale)
    share = 1.0 / jnp.sum(weights, -1, keepdims=True)
    acc = jnp.dot(weights.astype(jnp.bfloat16), piece(2), preferred_element_type=jnp.float32)
    result = (acc * share).reshape(slots, rows, size)
    for slot, device in enumerate(order):
        out_ref[slot] = result[device].astype(jnp.bfloat16)


def unpack_kernel(places, in_ref, out_ref):
    size = in_ref.shape[-1]
    for head, slot in enumerate(places):
        out_ref[0, :, head * size:(head + 1) * size] = in_ref[slot]


def shards(groups, ranks, queries, keys, values, span_index):
    rows, width = queries.shape[1:]
    size = width // HEADS
    slots = groups * ranks
    heads, places = slot_heads(slots)
    order = way_back(groups, ranks)
    vmem = pl.BlockSpec(memory_space=pltpu.VMEM)
    smem = pl.BlockSpec(memory_space=pltpu.SMEM)
    hbm = pl.BlockSpec(memory_space=pltpu.HBM)
    queries, keys, values = [
        pltpu.with_memory_space_constraint(a, pltpu.HBM) for a in (queries, keys, values)
    ]
    params = pltpu.CompilerParams(vmem_limit_bytes=32 * 2**20)
    span_index = pltpu.with_memory_space_constraint(span_index, pltpu.HBM)
    packed, bias = pl.pallas_call(
        functools.partial(pack_kernel, heads),
        out_shape=[
            jax.ShapeDtypeStruct((slots, 3, rows, size), jnp.bfloat16),
            jax.ShapeDtypeStruct((groups, slots * rows), jnp.float32),
        ],
        in_specs=[hbm] * 4,
        out_specs=[vmem] * 2,
        scratch_shapes=[
            pltpu.VMEM((3, rows, width), jnp.bfloat16),
            pltpu.SMEM((groups,), jnp.int32),
            pltpu.SemaphoreType.DMA((4,)),
        ],
        compiler_params=params,
    )(queries, keys, values, span_index)
    whole = lax.all_to_all(packed, AXES, 0, 0, tiled=True)
    pair = groups == 2
    done = pl.pallas_call(
        functools.partial(attend_pair_kernel if pair else attend_kernel, order, groups),
        out_shape=jax.ShapeDtypeStruct((slots, rows, size), jnp.bfloat16),
        in_specs=[vmem if pair else smem, vmem],
        out_specs=vmem,
        compiler_params=params,
    )(bias if pair else span_index, whole)
    back = lax.all_to_all(done, AXES, 0, 0, axis_index_groups=[order], tiled=True)
    return pl.pallas_call(
        functools.partial(unpack_kernel, [order.index(p) for p in places]),
        out_shape=jax.ShapeDtypeStruct((1, rows, width), jnp.bfloat16),
        in_specs=[vmem],
        out_specs=vmem,
        compiler_params=params,
    )(back)


def solution(mesh):
    spec = P("span", "seq", None)
    body = functools.partial(shards, mesh.shape["span"], mesh.shape["seq"])
    return jax.shard_map(body, mesh=mesh, in_specs=(spec, spec, spec, P()), out_specs=spec, check_vma=False)
```

```python
import functools
import math

import jax
import jax.numpy as jnp
from jax import lax
from jax.experimental import pallas as pl
from jax.experimental.pallas import tpu as pltpu
from jax.sharding import PartitionSpec as P

HEADS = 20
MASKED = -1e30
AXES = ("span", "seq")


def slot_heads(slots):
    spread = [d for d in range(slots) if d % 2 == 0] + [d for d in range(slots) if d % 2]
    heads = [0] * slots
    for place, d in enumerate(spread):
        heads[d] = place % HEADS
    return heads, spread[:HEADS]


def rank_order(groups, ranks):
    per = [r for c in range(2) for y in range(2) for r in range(ranks) if r % 4 == 2 * y + c]
    return [g * ranks + r for g in range(groups) for r in per]


def pack_kernel(heads, q_hbm, k_hbm, v_hbm, span_hbm, out_ref, bias_ref, held, spans, sems):
    copies = [
        pltpu.make_async_copy(src, held.at[pl.ds(i, 1)], sems.at[i])
        for i, src in enumerate((q_hbm, k_hbm, v_hbm))
    ]
    index = pltpu.make_async_copy(span_hbm, spans, sems.at[3])
    index.start()
    for c in copies:
        c.start()
    size = out_ref.shape[-1]
    for i, c in enumerate(copies):
        c.wait()
        for slot, head in enumerate(heads):
            out_ref[slot, i] = held[i, :, head * size:(head + 1) * size]
    index.wait()
    groups, tokens = bias_ref.shape
    key_group = lax.broadcasted_iota(jnp.int32, (1, tokens), 1) // (tokens // groups)
    for group in range(groups):
        seen = key_group == group
        for p in range(groups):
            seen |= (key_group == p) & (spans[p] == spans[group] - 1)
        bias_ref[group:group + 1] = jnp.where(seen, 0.0, MASKED)


def attend_kernel(groups, span_ref, in_ref, out_ref):
    slots, _, rows, size = in_ref.shape
    per = slots // groups
    tokens = per * rows
    scale = size ** -0.5

    def piece(part, group):
        block = in_ref[pl.ds(group * per, per), part].astype(jnp.float32)
        return block.reshape(tokens, size).astype(jnp.bfloat16)

    def one(group, carry):
        mine = span_ref[group]
        source = jnp.int32(0)
        found = jnp.int32(0)
        for p in range(groups):
            hit = (span_ref[p] == mine - 1).astype(jnp.int32)
            source = source + hit * p
            found = found + hit
        has = found > 0
        q = piece(0, group)
        dims = (((1,), (1,)), ((), ()))
        own = lax.dot_general(q, piece(1, group), dims, preferred_element_type=jnp.float32) * scale
        before = lax.dot_general(q, piece(1, source), dims, preferred_element_type=jnp.float32) * scale
        before = jnp.where(has, before, -1e30)
        top = jnp.maximum(jnp.max(own, -1, keepdims=True), jnp.max(before, -1, keepdims=True))
        own_w = jnp.exp(own - top)
        before_w = jnp.where(has, jnp.exp(before - top), 0.0)
        total = jnp.sum(own_w, -1, keepdims=True) + jnp.sum(before_w, -1, keepdims=True)
        acc = jnp.dot(own_w.astype(jnp.bfloat16), piece(2, group), preferred_element_type=jnp.float32)
        acc += jnp.dot(before_w.astype(jnp.bfloat16), piece(2, source), preferred_element_type=jnp.float32)
        result = (acc / total).reshape(per, rows, size).astype(jnp.bfloat16)
        out_ref[pl.ds(group * per, per)] = result
        return carry

    lax.fori_loop(0, groups, one, 0)


def attend_pair_kernel(bias_ref, in_ref, out_ref):
    slots, _, rows, size = in_ref.shape
    half = slots * rows // 2

    def piece(part):
        return in_ref[:, part].reshape(-1, size)

    scores = lax.dot_general(
        piece(0), piece(1), (((1,), (1,)), ((), ())), preferred_element_type=jnp.float32
    )
    scores = jnp.concatenate([scores[:half] + bias_ref[0:1], scores[half:] + bias_ref[1:2]], 0)
    scale = size ** -0.5 * math.log2(math.e)
    weights = jnp.exp2((scores - jnp.max(scores, -1, keepdims=True)) * scale)
    share = 1.0 / jnp.sum(weights, -1, keepdims=True)
    acc = jnp.dot(weights.astype(jnp.bfloat16), piece(2), preferred_element_type=jnp.float32)
    out_ref[...] = (acc * share).reshape(slots, rows, size).astype(jnp.bfloat16)


def unpack_kernel(places, in_ref, out_ref):
    size = in_ref.shape[-1]
    for head, slot in enumerate(places):
        out_ref[0, :, head * size:(head + 1) * size] = in_ref[slot]


def shards(groups, ranks, queries, keys, values, span_index):
    rows, width = queries.shape[1:]
    size = width // HEADS
    slots = groups * ranks
    heads, places = slot_heads(slots)
    order = [rank_order(groups, ranks)] if ranks % 4 == 0 else None
    vmem = pl.BlockSpec(memory_space=pltpu.VMEM)
    smem = pl.BlockSpec(memory_space=pltpu.SMEM)
    hbm = pl.BlockSpec(memory_space=pltpu.HBM)
    queries, keys, values = [
        pltpu.with_memory_space_constraint(a, pltpu.HBM) for a in (queries, keys, values)
    ]
    params = pltpu.CompilerParams(vmem_limit_bytes=32 * 2**20)
    span_index = pltpu.with_memory_space_constraint(span_index, pltpu.HBM)
    packed, bias = pl.pallas_call(
        functools.partial(pack_kernel, heads),
        out_shape=[
            jax.ShapeDtypeStruct((slots, 3, rows, size), jnp.bfloat16),
            jax.ShapeDtypeStruct((groups, slots * rows), jnp.float32),
        ],
        in_specs=[hbm] * 4,
        out_specs=[vmem] * 2,
        scratch_shapes=[
            pltpu.VMEM((3, rows, width), jnp.bfloat16),
            pltpu.SMEM((groups,), jnp.int32),
            pltpu.SemaphoreType.DMA((4,)),
        ],
        compiler_params=params,
    )(queries, keys, values, span_index)
    whole = lax.all_to_all(packed, AXES, 0, 0, axis_index_groups=order, tiled=True)
    pair = groups == 2
    done = pl.pallas_call(
        attend_pair_kernel if pair else functools.partial(attend_kernel, groups),
        out_shape=jax.ShapeDtypeStruct((slots, rows, size), jnp.bfloat16),
        in_specs=[vmem if pair else smem, vmem],
        out_specs=vmem,
        compiler_params=params,
    )(bias if pair else span_index, whole)
    back = lax.all_to_all(done, AXES, 0, 0, axis_index_groups=order, tiled=True)
    return pl.pallas_call(
        functools.partial(unpack_kernel, places),
        out_shape=jax.ShapeDtypeStruct((1, rows, width), jnp.bfloat16),
        in_specs=[vmem],
        out_specs=vmem,
        compiler_params=params,
    )(back)


def solution(mesh):
    spec = P("span", "seq", None)
    body = functools.partial(shards, mesh.shape["span"], mesh.shape["seq"])
    return jax.shard_map(body, mesh=mesh, in_specs=(spec, spec, spec, P()), out_specs=spec, check_vma=False)
```

```python
import functools
import math

import jax
import jax.numpy as jnp
from jax import lax
from jax.experimental import pallas as pl
from jax.experimental.pallas import tpu as pltpu
from jax.sharding import PartitionSpec as P

HEADS = 20
MASKED = -1e30
AXES = ("span", "seq")


def slot_heads(slots):
    spread = [d for d in range(slots) if d % 2 == 0] + [d for d in range(slots) if d % 2]
    heads = [0] * slots
    for place, d in enumerate(spread):
        heads[d] = place % HEADS
    return heads, spread[:HEADS]


def rank_order(groups, ranks):
    per = [r for c in range(2) for y in range(2) for r in range(ranks) if r % 4 == 2 * y + c]
    if groups == 2:
        return [g * ranks + r for r in per for g in range(groups)]
    return [g * ranks + r for g in range(groups) for r in per]


def pack_kernel(heads, q_hbm, k_hbm, v_hbm, span_hbm, out_ref, bias_ref, held, spans, sems):
    copies = [
        pltpu.make_async_copy(src, held.at[pl.ds(i, 1)], sems.at[i])
        for i, src in enumerate((q_hbm, k_hbm, v_hbm))
    ]
    index = pltpu.make_async_copy(span_hbm, spans, sems.at[3])
    index.start()
    for c in copies:
        c.start()
    size = out_ref.shape[-1]
    for i, c in enumerate(copies):
        c.wait()
        for slot, head in enumerate(heads):
            out_ref[slot, i] = held[i, :, head * size:(head + 1) * size]
    index.wait()
    groups, tokens = bias_ref.shape
    rows = held.shape[1]
    key_group = lax.broadcasted_iota(jnp.int32, (1, tokens), 1) // rows % groups
    for group in range(groups):
        seen = key_group == group
        for p in range(groups):
            seen |= (key_group == p) & (spans[p] == spans[group] - 1)
        bias_ref[group:group + 1] = jnp.where(seen, 0.0, MASKED)


def attend_kernel(groups, span_ref, in_ref, out_ref):
    slots, _, rows, size = in_ref.shape
    per = slots // groups
    tokens = per * rows
    scale = size ** -0.5

    def piece(part, group):
        block = in_ref[pl.ds(group * per, per), part].astype(jnp.float32)
        return block.reshape(tokens, size).astype(jnp.bfloat16)

    def one(group, carry):
        mine = span_ref[group]
        source = jnp.int32(0)
        found = jnp.int32(0)
        for p in range(groups):
            hit = (span_ref[p] == mine - 1).astype(jnp.int32)
            source = source + hit * p
            found = found + hit
        has = found > 0
        q = piece(0, group)
        dims = (((1,), (1,)), ((), ()))
        own = lax.dot_general(q, piece(1, group), dims, preferred_element_type=jnp.float32) * scale
        before = lax.dot_general(q, piece(1, source), dims, preferred_element_type=jnp.float32) * scale
        before = jnp.where(has, before, -1e30)
        top = jnp.maximum(jnp.max(own, -1, keepdims=True), jnp.max(before, -1, keepdims=True))
        own_w = jnp.exp(own - top)
        before_w = jnp.where(has, jnp.exp(before - top), 0.0)
        total = jnp.sum(own_w, -1, keepdims=True) + jnp.sum(before_w, -1, keepdims=True)
        acc = jnp.dot(own_w.astype(jnp.bfloat16), piece(2, group), preferred_element_type=jnp.float32)
        acc += jnp.dot(before_w.astype(jnp.bfloat16), piece(2, source), preferred_element_type=jnp.float32)
        result = (acc / total).reshape(per, rows, size).astype(jnp.bfloat16)
        out_ref[pl.ds(group * per, per)] = result
        return carry

    lax.fori_loop(0, groups, one, 0)


def attend_pair_kernel(bias_ref, in_ref, out_ref):
    slots, _, rows, size = in_ref.shape

    def piece(part):
        return in_ref[:, part].reshape(-1, size)

    scores = lax.dot_general(
        piece(0), piece(1), (((1,), (1,)), ((), ())), preferred_element_type=jnp.float32
    )
    bias = [bias_ref[group:group + 1] for group in range(2)]
    scores = jnp.concatenate([scores[i * rows:(i + 1) * rows] + bias[i % 2] for i in range(slots)], 0)
    scale = size ** -0.5 * math.log2(math.e)
    weights = jnp.exp2((scores - jnp.max(scores, -1, keepdims=True)) * scale)
    share = 1.0 / jnp.sum(weights, -1, keepdims=True)
    acc = jnp.dot(weights.astype(jnp.bfloat16), piece(2), preferred_element_type=jnp.float32)
    out_ref[...] = (acc * share).reshape(slots, rows, size).astype(jnp.bfloat16)


def unpack_kernel(places, in_ref, out_ref):
    size = in_ref.shape[-1]
    for head, slot in enumerate(places):
        out_ref[0, :, head * size:(head + 1) * size] = in_ref[slot]


def shards(groups, ranks, queries, keys, values, span_index):
    rows, width = queries.shape[1:]
    size = width // HEADS
    slots = groups * ranks
    heads, places = slot_heads(slots)
    order = [rank_order(groups, ranks)] if ranks % 4 == 0 else None
    vmem = pl.BlockSpec(memory_space=pltpu.VMEM)
    smem = pl.BlockSpec(memory_space=pltpu.SMEM)
    hbm = pl.BlockSpec(memory_space=pltpu.HBM)
    queries, keys, values = [
        pltpu.with_memory_space_constraint(a, pltpu.HBM) for a in (queries, keys, values)
    ]
    params = pltpu.CompilerParams(vmem_limit_bytes=32 * 2**20)
    span_index = pltpu.with_memory_space_constraint(span_index, pltpu.HBM)
    packed, bias = pl.pallas_call(
        functools.partial(pack_kernel, heads),
        out_shape=[
            jax.ShapeDtypeStruct((slots, 3, rows, size), jnp.bfloat16),
            jax.ShapeDtypeStruct((groups, slots * rows), jnp.float32),
        ],
        in_specs=[hbm] * 4,
        out_specs=[vmem] * 2,
        scratch_shapes=[
            pltpu.VMEM((3, rows, width), jnp.bfloat16),
            pltpu.SMEM((groups,), jnp.int32),
            pltpu.SemaphoreType.DMA((4,)),
        ],
        compiler_params=params,
    )(queries, keys, values, span_index)
    whole = lax.all_to_all(packed, AXES, 0, 0, axis_index_groups=order, tiled=True)
    pair = groups == 2
    done = pl.pallas_call(
        attend_pair_kernel if pair else functools.partial(attend_kernel, groups),
        out_shape=jax.ShapeDtypeStruct((slots, rows, size), jnp.bfloat16),
        in_specs=[vmem if pair else smem, vmem],
        out_specs=vmem,
        compiler_params=params,
    )(bias if pair else span_index, whole)
    back = lax.all_to_all(done, AXES, 0, 0, axis_index_groups=order, tiled=True)
    return pl.pallas_call(
        functools.partial(unpack_kernel, places),
        out_shape=jax.ShapeDtypeStruct((1, rows, width), jnp.bfloat16),
        in_specs=[vmem],
        out_specs=vmem,
        compiler_params=params,
    )(back)


def solution(mesh):
    spec = P("span", "seq", None)
    body = functools.partial(shards, mesh.shape["span"], mesh.shape["seq"])
    return jax.shard_map(body, mesh=mesh, in_specs=(spec, spec, spec, P()), out_specs=spec, check_vma=False)
```

```python
import functools
import math

import jax
import jax.numpy as jnp
from jax import lax
from jax.experimental import pallas as pl
from jax.experimental.pallas import tpu as pltpu
from jax.sharding import PartitionSpec as P

HEADS = 20
MASKED = -1e30
AXES = ("span", "seq")


def slot_heads(slots):
    spread = [d for d in range(slots) if d % 2 == 0] + [d for d in range(slots) if d % 2]
    heads = [0] * slots
    for place, d in enumerate(spread):
        heads[d] = place % HEADS
    return heads, spread[:HEADS]


def rank_order(groups, ranks):
    if groups != 2:
        return list(range(groups * ranks))
    chips = [g * ranks + r for g in range(2) for y in (0, 2) for r in range(y, ranks, 4)]
    return chips + [d + 1 for d in chips[::-1]]


def pack_kernel(heads, q_hbm, k_hbm, v_hbm, span_hbm, out_ref, bias_ref, held, spans, sems):
    copies = [
        pltpu.make_async_copy(src, held.at[pl.ds(i, 1)], sems.at[i])
        for i, src in enumerate((q_hbm, k_hbm, v_hbm))
    ]
    index = pltpu.make_async_copy(span_hbm, spans, sems.at[3])
    index.start()
    for c in copies:
        c.start()
    size = out_ref.shape[-1]
    for i, c in enumerate(copies):
        c.wait()
        for slot, head in enumerate(heads):
            out_ref[slot, i] = held[i, :, head * size:(head + 1) * size]
    index.wait()
    groups, tokens = bias_ref.shape
    place = lax.broadcasted_iota(jnp.int32, (1, tokens), 1)
    key_group = (place + tokens // 4) // (tokens // 2) % 2
    for group in range(groups):
        seen = key_group == group
        for p in range(groups):
            seen |= (key_group == p) & (spans[p] == spans[group] - 1)
        bias_ref[group:group + 1] = jnp.where(seen, 0.0, MASKED)


def attend_kernel(groups, span_ref, in_ref, out_ref):
    slots, _, rows, size = in_ref.shape
    per = slots // groups
    tokens = per * rows
    scale = size ** -0.5

    def piece(part, group):
        block = in_ref[pl.ds(group * per, per), part].astype(jnp.float32)
        return block.reshape(tokens, size).astype(jnp.bfloat16)

    def one(group, carry):
        mine = span_ref[group]
        source = jnp.int32(0)
        found = jnp.int32(0)
        for p in range(groups):
            hit = (span_ref[p] == mine - 1).astype(jnp.int32)
            source = source + hit * p
            found = found + hit
        has = found > 0
        q = piece(0, group)
        dims = (((1,), (1,)), ((), ()))
        own = lax.dot_general(q, piece(1, group), dims, preferred_element_type=jnp.float32) * scale
        before = lax.dot_general(q, piece(1, source), dims, preferred_element_type=jnp.float32) * scale
        before = jnp.where(has, before, -1e30)
        top = jnp.maximum(jnp.max(own, -1, keepdims=True), jnp.max(before, -1, keepdims=True))
        own_w = jnp.exp(own - top)
        before_w = jnp.where(has, jnp.exp(before - top), 0.0)
        total = jnp.sum(own_w, -1, keepdims=True) + jnp.sum(before_w, -1, keepdims=True)
        acc = jnp.dot(own_w.astype(jnp.bfloat16), piece(2, group), preferred_element_type=jnp.float32)
        acc += jnp.dot(before_w.astype(jnp.bfloat16), piece(2, source), preferred_element_type=jnp.float32)
        result = (acc / total).reshape(per, rows, size).astype(jnp.bfloat16)
        out_ref[pl.ds(group * per, per)] = result
        return carry

    lax.fori_loop(0, groups, one, 0)


def attend_pair_kernel(bias_ref, in_ref, out_ref):
    slots, _, rows, size = in_ref.shape
    quarter = slots * rows // 4

    def piece(part):
        return in_ref[:, part].reshape(-1, size)

    scores = lax.dot_general(
        piece(0), piece(1), (((1,), (1,)), ((), ())), preferred_element_type=jnp.float32
    )
    scores = jnp.concatenate(
        [
            scores[i * quarter:(i + 1) * quarter] + bias_ref[group:group + 1]
            for i, group in enumerate((0, 1, 1, 0))
        ],
        0,
    )
    scale = size ** -0.5 * math.log2(math.e)
    weights = jnp.exp2((scores - jnp.max(scores, -1, keepdims=True)) * scale)
    share = 1.0 / jnp.sum(weights, -1, keepdims=True)
    acc = jnp.dot(weights.astype(jnp.bfloat16), piece(2), preferred_element_type=jnp.float32)
    out_ref[...] = (acc * share).reshape(slots, rows, size).astype(jnp.bfloat16)


def unpack_kernel(places, in_ref, out_ref):
    size = in_ref.shape[-1]
    for head, slot in enumerate(places):
        out_ref[0, :, head * size:(head + 1) * size] = in_ref[slot]


def shards(groups, ranks, queries, keys, values, span_index):
    rows, width = queries.shape[1:]
    size = width // HEADS
    slots = groups * ranks
    heads, places = slot_heads(slots)
    order = [rank_order(groups, ranks)] if ranks % 4 == 0 else None
    vmem = pl.BlockSpec(memory_space=pltpu.VMEM)
    smem = pl.BlockSpec(memory_space=pltpu.SMEM)
    hbm = pl.BlockSpec(memory_space=pltpu.HBM)
    queries, keys, values = [
        pltpu.with_memory_space_constraint(a, pltpu.HBM) for a in (queries, keys, values)
    ]
    params = pltpu.CompilerParams(vmem_limit_bytes=32 * 2**20)
    span_index = pltpu.with_memory_space_constraint(span_index, pltpu.HBM)
    packed, bias = pl.pallas_call(
        functools.partial(pack_kernel, heads),
        out_shape=[
            jax.ShapeDtypeStruct((slots, 3, rows, size), jnp.bfloat16),
            jax.ShapeDtypeStruct((groups, slots * rows), jnp.float32),
        ],
        in_specs=[hbm] * 4,
        out_specs=[vmem] * 2,
        scratch_shapes=[
            pltpu.VMEM((3, rows, width), jnp.bfloat16),
            pltpu.SMEM((groups,), jnp.int32),
            pltpu.SemaphoreType.DMA((4,)),
        ],
        compiler_params=params,
    )(queries, keys, values, span_index)
    whole = lax.all_to_all(packed, AXES, 0, 0, axis_index_groups=order, tiled=True)
    pair = groups == 2
    done = pl.pallas_call(
        attend_pair_kernel if pair else functools.partial(attend_kernel, groups),
        out_shape=jax.ShapeDtypeStruct((slots, rows, size), jnp.bfloat16),
        in_specs=[vmem if pair else smem, vmem],
        out_specs=vmem,
        compiler_params=params,
    )(bias if pair else span_index, whole)
    back = lax.all_to_all(done, AXES, 0, 0, axis_index_groups=order, tiled=True)
    return pl.pallas_call(
        functools.partial(unpack_kernel, places),
        out_shape=jax.ShapeDtypeStruct((1, rows, width), jnp.bfloat16),
        in_specs=[vmem],
        out_specs=vmem,
        compiler_params=params,
    )(back)


def solution(mesh):
    spec = P("span", "seq", None)
    body = functools.partial(shards, mesh.shape["span"], mesh.shape["seq"])
    return jax.shard_map(body, mesh=mesh, in_specs=(spec, spec, spec, P()), out_specs=spec, check_vma=False)
```

```python
import functools
import math

import jax
import jax.numpy as jnp
from jax import lax
from jax.experimental import pallas as pl
from jax.experimental.pallas import tpu as pltpu
from jax.sharding import PartitionSpec as P

HEADS = 20
MASKED = -1e30
AXES = ("span", "seq")


def rank_order(groups, ranks):
    per = [r for c in range(2) for y in range(2) for r in range(ranks) if r % 4 == 2 * y + c]
    return [g * ranks + r for g in range(groups) for r in per]


def pack_kernel(q_hbm, k_hbm, v_hbm, span_hbm, out_ref, bias_ref, spans, sems, span_sem):
    slots = out_ref.shape[0]
    copies = []
    for i, src in enumerate((q_hbm, k_hbm, v_hbm)):
        for n, first in enumerate(range(0, slots, HEADS)):
            count = min(HEADS, slots - first)
            copies.append(
                pltpu.make_async_copy(
                    src.at[pl.ds(0, count)], out_ref.at[pl.ds(first, count), i], sems.at[i, n]
                )
            )
    index = pltpu.make_async_copy(span_hbm, spans, span_sem)
    for c in copies:
        c.start()
    index.start()
    index.wait()
    groups, tokens = bias_ref.shape
    key_group = lax.broadcasted_iota(jnp.int32, (1, tokens), 1) // (tokens // groups)
    for group in range(groups):
        seen = key_group == group
        for p in range(groups):
            seen |= (key_group == p) & (spans[p] == spans[group] - 1)
        bias_ref[group:group + 1] = jnp.where(seen, 0.0, MASKED)
    for c in copies:
        c.wait()


def attend_kernel(groups, span_ref, in_ref, out_ref):
    slots, _, rows, size = in_ref.shape
    per = slots // groups
    tokens = per * rows
    scale = size ** -0.5

    def piece(part, group):
        block = in_ref[pl.ds(group * per, per), part].astype(jnp.float32)
        return block.reshape(tokens, size).astype(jnp.bfloat16)

    def one(group, carry):
        mine = span_ref[group]
        source = jnp.int32(0)
        found = jnp.int32(0)
        for p in range(groups):
            hit = (span_ref[p] == mine - 1).astype(jnp.int32)
            source = source + hit * p
            found = found + hit
        has = found > 0
        q = piece(0, group)
        dims = (((1,), (1,)), ((), ()))
        own = lax.dot_general(q, piece(1, group), dims, preferred_element_type=jnp.float32) * scale
        before = lax.dot_general(q, piece(1, source), dims, preferred_element_type=jnp.float32) * scale
        before = jnp.where(has, before, -1e30)
        top = jnp.maximum(jnp.max(own, -1, keepdims=True), jnp.max(before, -1, keepdims=True))
        own_w = jnp.exp(own - top)
        before_w = jnp.where(has, jnp.exp(before - top), 0.0)
        total = jnp.sum(own_w, -1, keepdims=True) + jnp.sum(before_w, -1, keepdims=True)
        acc = jnp.dot(own_w.astype(jnp.bfloat16), piece(2, group), preferred_element_type=jnp.float32)
        acc += jnp.dot(before_w.astype(jnp.bfloat16), piece(2, source), preferred_element_type=jnp.float32)
        result = (acc / total).reshape(per, rows, size).astype(jnp.bfloat16)
        out_ref[pl.ds(group * per, per)] = result
        return carry

    lax.fori_loop(0, groups, one, 0)


def attend_pair_kernel(bias_ref, in_ref, out_ref):
    slots, _, rows, size = in_ref.shape
    half = slots * rows // 2

    def piece(part):
        return in_ref[:, part].reshape(-1, size)

    scores = lax.dot_general(
        piece(0), piece(1), (((1,), (1,)), ((), ())), preferred_element_type=jnp.float32
    )
    scores = jnp.concatenate([scores[:half] + bias_ref[0:1], scores[half:] + bias_ref[1:2]], 0)
    scale = size ** -0.5 * math.log2(math.e)
    weights = jnp.exp2((scores - jnp.max(scores, -1, keepdims=True)) * scale)
    share = 1.0 / jnp.sum(weights, -1, keepdims=True)
    acc = jnp.dot(weights.astype(jnp.bfloat16), piece(2), preferred_element_type=jnp.float32)
    out_ref[...] = (acc * share).reshape(slots, rows, size).astype(jnp.bfloat16)


def unpack_kernel(in_ref, out_hbm, sem):
    copy = pltpu.make_async_copy(in_ref.at[pl.ds(0, HEADS)], out_hbm, sem)
    copy.start()
    copy.wait()


def by_head(x):
    return x.reshape(x.shape[1], HEADS, -1).transpose(1, 0, 2)


def shards(groups, ranks, queries, keys, values, span_index):
    rows, width = queries.shape[1:]
    size = width // HEADS
    slots = groups * ranks
    order = [rank_order(groups, ranks)] if ranks % 4 == 0 else None
    vmem = pl.BlockSpec(memory_space=pltpu.VMEM)
    smem = pl.BlockSpec(memory_space=pltpu.SMEM)
    hbm = pl.BlockSpec(memory_space=pltpu.HBM)
    queries, keys, values = [
        pltpu.with_memory_space_constraint(by_head(a), pltpu.HBM) for a in (queries, keys, values)
    ]
    params = pltpu.CompilerParams(vmem_limit_bytes=32 * 2**20)
    span_index = pltpu.with_memory_space_constraint(span_index, pltpu.HBM)
    packed, bias = pl.pallas_call(
        pack_kernel,
        out_shape=[
            jax.ShapeDtypeStruct((slots, 3, rows, size), jnp.bfloat16),
            jax.ShapeDtypeStruct((groups, slots * rows), jnp.float32),
        ],
        in_specs=[hbm] * 4,
        out_specs=[vmem] * 2,
        scratch_shapes=[
            pltpu.SMEM((groups,), jnp.int32),
            pltpu.SemaphoreType.DMA((3, -(-slots // HEADS))),
            pltpu.SemaphoreType.DMA(()),
        ],
        compiler_params=params,
    )(queries, keys, values, span_index)
    whole = lax.all_to_all(packed, AXES, 0, 0, axis_index_groups=order, tiled=True)
    pair = groups == 2
    done = pl.pallas_call(
        attend_pair_kernel if pair else functools.partial(attend_kernel, groups),
        out_shape=jax.ShapeDtypeStruct((slots, rows, size), jnp.bfloat16),
        in_specs=[vmem if pair else smem, vmem],
        out_specs=vmem,
        compiler_params=params,
    )(bias if pair else span_index, whole)
    back = lax.all_to_all(done, AXES, 0, 0, axis_index_groups=order, tiled=True)
    result = pl.pallas_call(
        unpack_kernel,
        out_shape=jax.ShapeDtypeStruct((HEADS, rows, size), jnp.bfloat16),
        in_specs=[vmem],
        out_specs=hbm,
        scratch_shapes=[pltpu.SemaphoreType.DMA(())],
        compiler_params=params,
    )(back)
    return result.transpose(1, 0, 2).reshape(1, rows, width)


def solution(mesh):
    spec = P("span", "seq", None)
    body = functools.partial(shards, mesh.shape["span"], mesh.shape["seq"])
    return jax.shard_map(body, mesh=mesh, in_specs=(spec, spec, spec, P()), out_specs=spec, check_vma=False)
```

```python
import functools
import math

import jax
import jax.numpy as jnp
from jax import lax
from jax.experimental import pallas as pl
from jax.experimental.pallas import tpu as pltpu
from jax.sharding import PartitionSpec as P

HEADS = 20
MASKED = -1e30
AXES = ("span", "seq")


def slot_heads(slots):
    spread = [d for d in range(slots) if d % 2 == 0] + [d for d in range(slots) if d % 2]
    heads = [0] * slots
    for place, d in enumerate(spread):
        heads[d] = place % HEADS
    return heads, spread[:HEADS]


def rank_order(groups, ranks):
    per = [r for y in range(2) for c in range(2) for r in range(ranks) if r % 4 == 2 * y + c]
    return [g * ranks + r for g in range(groups) for r in per]


def pack_kernel(heads, q_hbm, k_hbm, v_hbm, span_hbm, out_ref, bias_ref, held, spans, sems):
    copies = [
        pltpu.make_async_copy(src, held.at[pl.ds(i, 1)], sems.at[i])
        for i, src in enumerate((q_hbm, k_hbm, v_hbm))
    ]
    index = pltpu.make_async_copy(span_hbm, spans, sems.at[3])
    index.start()
    for c in copies:
        c.start()
    size = out_ref.shape[-1]
    for i, c in enumerate(copies):
        c.wait()
        for slot, head in enumerate(heads):
            out_ref[slot, i] = held[i, :, head * size:(head + 1) * size]
    index.wait()
    groups, tokens = bias_ref.shape
    key_group = lax.broadcasted_iota(jnp.int32, (1, tokens), 1) // (tokens // groups)
    for group in range(groups):
        seen = key_group == group
        for p in range(groups):
            seen |= (key_group == p) & (spans[p] == spans[group] - 1)
        bias_ref[group:group + 1] = jnp.where(seen, 0.0, MASKED)


def attend_kernel(groups, span_ref, in_ref, out_ref):
    slots, _, rows, size = in_ref.shape
    per = slots // groups
    tokens = per * rows
    scale = size ** -0.5

    def piece(part, group):
        block = in_ref[pl.ds(group * per, per), part].astype(jnp.float32)
        return block.reshape(tokens, size).astype(jnp.bfloat16)

    def one(group, carry):
        mine = span_ref[group]
        source = jnp.int32(0)
        found = jnp.int32(0)
        for p in range(groups):
            hit = (span_ref[p] == mine - 1).astype(jnp.int32)
            source = source + hit * p
            found = found + hit
        has = found > 0
        q = piece(0, group)
        dims = (((1,), (1,)), ((), ()))
        own = lax.dot_general(q, piece(1, group), dims, preferred_element_type=jnp.float32) * scale
        before = lax.dot_general(q, piece(1, source), dims, preferred_element_type=jnp.float32) * scale
        before = jnp.where(has, before, -1e30)
        top = jnp.maximum(jnp.max(own, -1, keepdims=True), jnp.max(before, -1, keepdims=True))
        own_w = jnp.exp(own - top)
        before_w = jnp.where(has, jnp.exp(before - top), 0.0)
        total = jnp.sum(own_w, -1, keepdims=True) + jnp.sum(before_w, -1, keepdims=True)
        acc = jnp.dot(own_w.astype(jnp.bfloat16), piece(2, group), preferred_element_type=jnp.float32)
        acc += jnp.dot(before_w.astype(jnp.bfloat16), piece(2, source), preferred_element_type=jnp.float32)
        result = (acc / total).reshape(per, rows, size).astype(jnp.bfloat16)
        out_ref[pl.ds(group * per, per)] = result
        return carry

    lax.fori_loop(0, groups, one, 0)


def attend_pair_kernel(bias_ref, in_ref, out_ref):
    slots, _, rows, size = in_ref.shape
    half = slots * rows // 2

    def piece(part):
        return in_ref[:, part].reshape(-1, size)

    scores = lax.dot_general(
        piece(0), piece(1), (((1,), (1,)), ((), ())), preferred_element_type=jnp.float32
    )
    scores = jnp.concatenate([scores[:half] + bias_ref[0:1], scores[half:] + bias_ref[1:2]], 0)
    scale = size ** -0.5 * math.log2(math.e)
    weights = jnp.exp2((scores - jnp.max(scores, -1, keepdims=True)) * scale)
    share = 1.0 / jnp.sum(weights, -1, keepdims=True)
    acc = jnp.dot(weights.astype(jnp.bfloat16), piece(2), preferred_element_type=jnp.float32)
    out_ref[...] = (acc * share).reshape(slots, rows, size).astype(jnp.bfloat16)


def unpack_kernel(places, in_ref, out_ref):
    size = in_ref.shape[-1]
    for head, slot in enumerate(places):
        out_ref[0, :, head * size:(head + 1) * size] = in_ref[slot]


def shards(groups, ranks, queries, keys, values, span_index):
    rows, width = queries.shape[1:]
    size = width // HEADS
    slots = groups * ranks
    heads, places = slot_heads(slots)
    order = [rank_order(groups, ranks)] if ranks % 4 == 0 else None
    vmem = pl.BlockSpec(memory_space=pltpu.VMEM)
    smem = pl.BlockSpec(memory_space=pltpu.SMEM)
    hbm = pl.BlockSpec(memory_space=pltpu.HBM)
    queries, keys, values = [
        pltpu.with_memory_space_constraint(a, pltpu.HBM) for a in (queries, keys, values)
    ]
    params = pltpu.CompilerParams(vmem_limit_bytes=32 * 2**20)
    span_index = pltpu.with_memory_space_constraint(span_index, pltpu.HBM)
    packed, bias = pl.pallas_call(
        functools.partial(pack_kernel, heads),
        out_shape=[
            jax.ShapeDtypeStruct((slots, 3, rows, size), jnp.bfloat16),
            jax.ShapeDtypeStruct((groups, slots * rows), jnp.float32),
        ],
        in_specs=[hbm] * 4,
        out_specs=[vmem] * 2,
        scratch_shapes=[
            pltpu.VMEM((3, rows, width), jnp.bfloat16),
            pltpu.SMEM((groups,), jnp.int32),
            pltpu.SemaphoreType.DMA((4,)),
        ],
        compiler_params=params,
    )(queries, keys, values, span_index)
    whole = lax.all_to_all(packed, AXES, 0, 0, axis_index_groups=order, tiled=True)
    pair = groups == 2
    done = pl.pallas_call(
        attend_pair_kernel if pair else functools.partial(attend_kernel, groups),
        out_shape=jax.ShapeDtypeStruct((slots, rows, size), jnp.bfloat16),
        in_specs=[vmem if pair else smem, vmem],
        out_specs=vmem,
        compiler_params=params,
    )(bias if pair else span_index, whole)
    back = lax.all_to_all(done, AXES, 0, 0, axis_index_groups=order, tiled=True)
    return pl.pallas_call(
        functools.partial(unpack_kernel, places),
        out_shape=jax.ShapeDtypeStruct((1, rows, width), jnp.bfloat16),
        in_specs=[vmem],
        out_specs=vmem,
        compiler_params=params,
    )(back)


def solution(mesh):
    spec = P("span", "seq", None)
    body = functools.partial(shards, mesh.shape["span"], mesh.shape["seq"])
    return jax.shard_map(body, mesh=mesh, in_specs=(spec, spec, spec, P()), out_specs=spec, check_vma=False)
```

```python
import functools
import math

import jax
import jax.numpy as jnp
from jax import lax
from jax.experimental import pallas as pl
from jax.experimental.pallas import tpu as pltpu
from jax.sharding import PartitionSpec as P

HEADS = 20
MASKED = -1e30
AXES = ("span", "seq")


def slot_heads(slots):
    spread = [d for d in range(slots) if d % 2 == 0] + [d for d in range(slots) if d % 2]
    heads = [0] * slots
    for place, d in enumerate(spread):
        heads[d] = place % HEADS
    return heads, spread[:HEADS]


def rank_order(groups, ranks):
    per = [r for c in range(2) for y in range(2) for r in range(ranks) if r % 4 == 2 * y + c]
    return [g * ranks + r for g in range(groups) for r in per]


def pack_kernel(heads, q_hbm, k_hbm, v_hbm, out_ref, held, sems):
    copies = [
        pltpu.make_async_copy(src, held.at[pl.ds(i, 1)], sems.at[i])
        for i, src in enumerate((q_hbm, k_hbm, v_hbm))
    ]
    for c in copies:
        c.start()
    size = out_ref.shape[-1]
    for i, c in enumerate(copies):
        c.wait()
        for slot, head in enumerate(heads):
            out_ref[slot, i] = held[i, :, head * size:(head + 1) * size]


def attend_kernel(groups, span_ref, in_ref, out_ref):
    slots, _, rows, size = in_ref.shape
    per = slots // groups
    tokens = per * rows
    scale = size ** -0.5

    def piece(part, group):
        block = in_ref[pl.ds(group * per, per), part].astype(jnp.float32)
        return block.reshape(tokens, size).astype(jnp.bfloat16)

    def one(group, carry):
        mine = span_ref[group]
        source = jnp.int32(0)
        found = jnp.int32(0)
        for p in range(groups):
            hit = (span_ref[p] == mine - 1).astype(jnp.int32)
            source = source + hit * p
            found = found + hit
        has = found > 0
        q = piece(0, group)
        dims = (((1,), (1,)), ((), ()))
        own = lax.dot_general(q, piece(1, group), dims, preferred_element_type=jnp.float32) * scale
        before = lax.dot_general(q, piece(1, source), dims, preferred_element_type=jnp.float32) * scale
        before = jnp.where(has, before, -1e30)
        top = jnp.maximum(jnp.max(own, -1, keepdims=True), jnp.max(before, -1, keepdims=True))
        own_w = jnp.exp(own - top)
        before_w = jnp.where(has, jnp.exp(before - top), 0.0)
        total = jnp.sum(own_w, -1, keepdims=True) + jnp.sum(before_w, -1, keepdims=True)
        acc = jnp.dot(own_w.astype(jnp.bfloat16), piece(2, group), preferred_element_type=jnp.float32)
        acc += jnp.dot(before_w.astype(jnp.bfloat16), piece(2, source), preferred_element_type=jnp.float32)
        result = (acc / total).reshape(per, rows, size).astype(jnp.bfloat16)
        out_ref[pl.ds(group * per, per)] = result
        return carry

    lax.fori_loop(0, groups, one, 0)


def attend_pair_kernel(span_ref, in_ref, out_ref):
    slots, _, rows, size = in_ref.shape
    half = slots * rows // 2

    def piece(part):
        return in_ref[:, part].reshape(-1, size)

    scores = lax.dot_general(
        piece(0), piece(1), (((1,), (1,)), ((), ())), preferred_element_type=jnp.float32
    )
    spans = span_ref[...].reshape(1, 2)
    key_group = lax.broadcasted_iota(jnp.int32, (1, slots * rows), 1) // half
    bias = [
        jnp.where((key_group == group) | (spans[:, group:group + 1] == 1), 0.0, MASKED)
        for group in range(2)
    ]
    scores = jnp.concatenate([scores[:half] + bias[0], scores[half:] + bias[1]], 0)
    scale = size ** -0.5 * math.log2(math.e)
    weights = jnp.exp2((scores - jnp.max(scores, -1, keepdims=True)) * scale)
    share = 1.0 / jnp.sum(weights, -1, keepdims=True)
    acc = jnp.dot(weights.astype(jnp.bfloat16), piece(2), preferred_element_type=jnp.float32)
    out_ref[...] = (acc * share).reshape(slots, rows, size).astype(jnp.bfloat16)


def unpack_kernel(places, in_ref, out_ref):
    size = in_ref.shape[-1]
    for head, slot in enumerate(places):
        out_ref[0, :, head * size:(head + 1) * size] = in_ref[slot]


def shards(groups, ranks, queries, keys, values, span_index):
    rows, width = queries.shape[1:]
    size = width // HEADS
    slots = groups * ranks
    heads, places = slot_heads(slots)
    order = [rank_order(groups, ranks)] if ranks % 4 == 0 else None
    vmem = pl.BlockSpec(memory_space=pltpu.VMEM)
    smem = pl.BlockSpec(memory_space=pltpu.SMEM)
    hbm = pl.BlockSpec(memory_space=pltpu.HBM)
    queries, keys, values = [
        pltpu.with_memory_space_constraint(a, pltpu.HBM) for a in (queries, keys, values)
    ]
    params = pltpu.CompilerParams(vmem_limit_bytes=32 * 2**20)
    packed = pl.pallas_call(
        functools.partial(pack_kernel, heads),
        out_shape=jax.ShapeDtypeStruct((slots, 3, rows, size), jnp.bfloat16),
        in_specs=[hbm] * 3,
        out_specs=vmem,
        scratch_shapes=[pltpu.VMEM((3, rows, width), jnp.bfloat16), pltpu.SemaphoreType.DMA((3,))],
        compiler_params=params,
    )(queries, keys, values)
    whole = lax.all_to_all(packed, AXES, 0, 0, axis_index_groups=order, tiled=True)
    pair = groups == 2
    done = pl.pallas_call(
        attend_pair_kernel if pair else functools.partial(attend_kernel, groups),
        out_shape=jax.ShapeDtypeStruct((slots, rows, size), jnp.bfloat16),
        in_specs=[vmem if pair else smem, vmem],
        out_specs=vmem,
        compiler_params=params,
    )(span_index, whole)
    back = lax.all_to_all(done, AXES, 0, 0, axis_index_groups=order, tiled=True)
    return pl.pallas_call(
        functools.partial(unpack_kernel, places),
        out_shape=jax.ShapeDtypeStruct((1, rows, width), jnp.bfloat16),
        in_specs=[vmem],
        out_specs=vmem,
        compiler_params=params,
    )(back)


def solution(mesh):
    spec = P("span", "seq", None)
    body = functools.partial(shards, mesh.shape["span"], mesh.shape["seq"])
    return jax.shard_map(body, mesh=mesh, in_specs=(spec, spec, spec, P()), out_specs=spec, check_vma=False)
```

```python
import functools
import math

import jax
import jax.numpy as jnp
from jax import lax
from jax.experimental import pallas as pl
from jax.experimental.pallas import tpu as pltpu
from jax.sharding import PartitionSpec as P

HEADS = 20
MASKED = -1e30
AXES = ("span", "seq")


def slot_heads(slots):
    spread = [d for d in range(slots) if d % 2 == 0] + [d for d in range(slots) if d % 2]
    heads = [0] * slots
    for place, d in enumerate(spread):
        heads[d] = place % HEADS
    return heads, spread[:HEADS]


def rank_order(groups, ranks):
    per = [r for c in range(2) for y in range(2) for r in range(ranks) if r % 4 == 2 * y + c]
    return [g * ranks + r for g in range(groups) for r in per]


def pack_kernel(heads, q_hbm, k_hbm, v_hbm, span_hbm, out_ref, bias_ref, held, spans, sems):
    copies = [
        pltpu.make_async_copy(src, held.at[pl.ds(i, 1)], sems.at[i])
        for i, src in enumerate((q_hbm, k_hbm, v_hbm))
    ]
    index = pltpu.make_async_copy(span_hbm, spans, sems.at[3])
    index.start()
    for c in copies:
        c.start()
    size = out_ref.shape[-1]
    for i, c in enumerate(copies):
        c.wait()
        for slot, head in enumerate(heads):
            out_ref[slot, i] = held[i, :, head * size:(head + 1) * size]
    index.wait()
    groups, tokens = bias_ref.shape
    key_group = lax.broadcasted_iota(jnp.int32, (1, tokens), 1) // (tokens // groups)
    for group in range(groups):
        seen = key_group == group
        for p in range(groups):
            seen |= (key_group == p) & (spans[p] == spans[group] - 1)
        bias_ref[group:group + 1] = jnp.where(seen, 0.0, MASKED)


def attend_kernel(groups, span_ref, in_ref, out_ref):
    slots, _, rows, size = in_ref.shape
    per = slots // groups
    tokens = per * rows
    scale = size ** -0.5

    def piece(part, group):
        block = in_ref[pl.ds(group * per, per), part].astype(jnp.float32)
        return block.reshape(tokens, size).astype(jnp.bfloat16)

    def one(group, carry):
        mine = span_ref[group]
        source = jnp.int32(0)
        found = jnp.int32(0)
        for p in range(groups):
            hit = (span_ref[p] == mine - 1).astype(jnp.int32)
            source = source + hit * p
            found = found + hit
        has = found > 0
        q = piece(0, group)
        dims = (((1,), (1,)), ((), ()))
        own = lax.dot_general(q, piece(1, group), dims, preferred_element_type=jnp.float32) * scale
        before = lax.dot_general(q, piece(1, source), dims, preferred_element_type=jnp.float32) * scale
        before = jnp.where(has, before, -1e30)
        top = jnp.maximum(jnp.max(own, -1, keepdims=True), jnp.max(before, -1, keepdims=True))
        own_w = jnp.exp(own - top)
        before_w = jnp.where(has, jnp.exp(before - top), 0.0)
        total = jnp.sum(own_w, -1, keepdims=True) + jnp.sum(before_w, -1, keepdims=True)
        acc = jnp.dot(own_w.astype(jnp.bfloat16), piece(2, group), preferred_element_type=jnp.float32)
        acc += jnp.dot(before_w.astype(jnp.bfloat16), piece(2, source), preferred_element_type=jnp.float32)
        result = (acc / total).reshape(per, rows, size).astype(jnp.bfloat16)
        out_ref[pl.ds(group * per, per)] = result
        return carry

    lax.fori_loop(0, groups, one, 0)


def attend_pair_kernel(order, bias_ref, in_ref, out_ref):
    slots, _, rows, size = in_ref.shape
    half = slots * rows // 2

    def piece(part):
        return in_ref[:, part].reshape(-1, size)

    scores = lax.dot_general(
        piece(0), piece(1), (((1,), (1,)), ((), ())), preferred_element_type=jnp.float32
    )
    scores = jnp.concatenate([scores[:half] + bias_ref[0:1], scores[half:] + bias_ref[1:2]], 0)
    scale = size ** -0.5 * math.log2(math.e)
    weights = jnp.exp2((scores - jnp.max(scores, -1, keepdims=True)) * scale)
    share = 1.0 / jnp.sum(weights, -1, keepdims=True)
    acc = jnp.dot(weights.astype(jnp.bfloat16), piece(2), preferred_element_type=jnp.float32)
    result = (acc * share).reshape(slots, rows, size)
    for slot, device in enumerate(order):
        out_ref[device] = result[slot].astype(jnp.bfloat16)


def unpack_kernel(places, in_ref, out_ref):
    size = in_ref.shape[-1]
    for head, slot in enumerate(places):
        out_ref[0, :, head * size:(head + 1) * size] = in_ref[slot]


def shards(groups, ranks, queries, keys, values, span_index):
    rows, width = queries.shape[1:]
    size = width // HEADS
    slots = groups * ranks
    heads, places = slot_heads(slots)
    order = [rank_order(groups, ranks)] if ranks % 4 == 0 else None
    vmem = pl.BlockSpec(memory_space=pltpu.VMEM)
    smem = pl.BlockSpec(memory_space=pltpu.SMEM)
    hbm = pl.BlockSpec(memory_space=pltpu.HBM)
    queries, keys, values = [
        pltpu.with_memory_space_constraint(a, pltpu.HBM) for a in (queries, keys, values)
    ]
    params = pltpu.CompilerParams(vmem_limit_bytes=32 * 2**20)
    span_index = pltpu.with_memory_space_constraint(span_index, pltpu.HBM)
    packed, bias = pl.pallas_call(
        functools.partial(pack_kernel, heads),
        out_shape=[
            jax.ShapeDtypeStruct((slots, 3, rows, size), jnp.bfloat16),
            jax.ShapeDtypeStruct((groups, slots * rows), jnp.float32),
        ],
        in_specs=[hbm] * 4,
        out_specs=[vmem] * 2,
        scratch_shapes=[
            pltpu.VMEM((3, rows, width), jnp.bfloat16),
            pltpu.SMEM((groups,), jnp.int32),
            pltpu.SemaphoreType.DMA((4,)),
        ],
        compiler_params=params,
    )(queries, keys, values, span_index)
    whole = lax.all_to_all(packed, AXES, 0, 0, axis_index_groups=order, tiled=True)
    pair = groups == 2
    done = pl.pallas_call(
        functools.partial(attend_pair_kernel, order[0]) if pair else functools.partial(attend_kernel, groups),
        out_shape=jax.ShapeDtypeStruct((slots, rows, size), jnp.bfloat16),
        in_specs=[vmem if pair else smem, vmem],
        out_specs=vmem,
        compiler_params=params,
    )(bias if pair else span_index, whole)
    back = lax.all_to_all(done, AXES, 0, 0, axis_index_groups=None if pair else order, tiled=True)
    return pl.pallas_call(
        functools.partial(unpack_kernel, [order[0][p] for p in places] if pair else places),
        out_shape=jax.ShapeDtypeStruct((1, rows, width), jnp.bfloat16),
        in_specs=[vmem],
        out_specs=vmem,
        compiler_params=params,
    )(back)


def solution(mesh):
    spec = P("span", "seq", None)
    body = functools.partial(shards, mesh.shape["span"], mesh.shape["seq"])
    return jax.shard_map(body, mesh=mesh, in_specs=(spec, spec, spec, P()), out_specs=spec, check_vma=False)
```

```python
import functools
import math

import jax
import jax.numpy as jnp
from jax import lax
from jax.experimental import pallas as pl
from jax.experimental.pallas import tpu as pltpu
from jax.sharding import PartitionSpec as P

HEADS = 20
MASKED = -1e30
AXES = ("span", "seq")


def slot_heads(slots):
    spread = [d for d in range(slots) if d % 2 == 0] + [d for d in range(slots) if d % 2]
    heads = [0] * slots
    for place, d in enumerate(spread):
        heads[d] = place % HEADS
    return heads, spread[:HEADS]


def rank_order(groups, ranks):
    per = [r for c in range(2) for y in range(2) for r in range(ranks) if r % 4 == 2 * y + c]
    return [g * ranks + r for g in range(groups) for r in per]


def pack_kernel(heads, q_hbm, k_hbm, v_hbm, out_ref, held, sems):
    copies = [
        pltpu.make_async_copy(src, held.at[pl.ds(i, 1)], sems.at[i])
        for i, src in enumerate((q_hbm, k_hbm, v_hbm))
    ]
    for c in copies:
        c.start(priority=1 if c is copies[1] else 0)
    size = out_ref.shape[-1]
    for i, c in enumerate(copies):
        c.wait()
        for slot, head in enumerate(heads):
            out_ref[slot, i] = held[i, :, head * size:(head + 1) * size]


def attend_kernel(groups, span_ref, in_ref, out_ref):
    slots, _, rows, size = in_ref.shape
    per = slots // groups
    tokens = per * rows
    scale = size ** -0.5

    def piece(part, group):
        block = in_ref[pl.ds(group * per, per), part].astype(jnp.float32)
        return block.reshape(tokens, size).astype(jnp.bfloat16)

    def one(group, carry):
        mine = span_ref[group]
        source = jnp.int32(0)
        found = jnp.int32(0)
        for p in range(groups):
            hit = (span_ref[p] == mine - 1).astype(jnp.int32)
            source = source + hit * p
            found = found + hit
        has = found > 0
        q = piece(0, group)
        dims = (((1,), (1,)), ((), ()))
        own = lax.dot_general(q, piece(1, group), dims, preferred_element_type=jnp.float32) * scale
        before = lax.dot_general(q, piece(1, source), dims, preferred_element_type=jnp.float32) * scale
        before = jnp.where(has, before, -1e30)
        top = jnp.maximum(jnp.max(own, -1, keepdims=True), jnp.max(before, -1, keepdims=True))
        own_w = jnp.exp(own - top)
        before_w = jnp.where(has, jnp.exp(before - top), 0.0)
        total = jnp.sum(own_w, -1, keepdims=True) + jnp.sum(before_w, -1, keepdims=True)
        acc = jnp.dot(own_w.astype(jnp.bfloat16), piece(2, group), preferred_element_type=jnp.float32)
        acc += jnp.dot(before_w.astype(jnp.bfloat16), piece(2, source), preferred_element_type=jnp.float32)
        result = (acc / total).reshape(per, rows, size).astype(jnp.bfloat16)
        out_ref[pl.ds(group * per, per)] = result
        return carry

    lax.fori_loop(0, groups, one, 0)


def attend_pair_kernel(span_ref, in_ref, out_ref):
    slots, _, rows, size = in_ref.shape
    half = slots * rows // 2

    def piece(part):
        return in_ref[:, part].reshape(-1, size)

    scores = lax.dot_general(
        piece(0), piece(1), (((1,), (1,)), ((), ())), preferred_element_type=jnp.float32
    )
    spans = span_ref[...].reshape(1, 2)
    key_group = lax.broadcasted_iota(jnp.int32, (1, slots * rows), 1) // half
    bias = [
        jnp.where((key_group == group) | (spans[:, group:group + 1] == 1), 0.0, MASKED)
        for group in range(2)
    ]
    scores = jnp.concatenate([scores[:half] + bias[0], scores[half:] + bias[1]], 0)
    scale = size ** -0.5 * math.log2(math.e)
    weights = jnp.exp2((scores - jnp.max(scores, -1, keepdims=True)) * scale)
    share = 1.0 / jnp.sum(weights, -1, keepdims=True)
    acc = jnp.dot(weights.astype(jnp.bfloat16), piece(2), preferred_element_type=jnp.float32)
    out_ref[...] = (acc * share).reshape(slots, rows, size).astype(jnp.bfloat16)


def unpack_kernel(places, in_ref, out_ref):
    size = in_ref.shape[-1]
    for head, slot in enumerate(places):
        out_ref[0, :, head * size:(head + 1) * size] = in_ref[slot]


def shards(groups, ranks, queries, keys, values, span_index):
    rows, width = queries.shape[1:]
    size = width // HEADS
    slots = groups * ranks
    heads, places = slot_heads(slots)
    order = [rank_order(groups, ranks)] if ranks % 4 == 0 else None
    vmem = pl.BlockSpec(memory_space=pltpu.VMEM)
    smem = pl.BlockSpec(memory_space=pltpu.SMEM)
    hbm = pl.BlockSpec(memory_space=pltpu.HBM)
    queries, keys, values = [
        pltpu.with_memory_space_constraint(a, pltpu.HBM) for a in (queries, keys, values)
    ]
    params = pltpu.CompilerParams(vmem_limit_bytes=32 * 2**20)
    packed = pl.pallas_call(
        functools.partial(pack_kernel, heads),
        out_shape=jax.ShapeDtypeStruct((slots, 3, rows, size), jnp.bfloat16),
        in_specs=[hbm] * 3,
        out_specs=vmem,
        scratch_shapes=[pltpu.VMEM((3, rows, width), jnp.bfloat16), pltpu.SemaphoreType.DMA((3,))],
        compiler_params=params,
    )(queries, keys, values)
    whole = lax.all_to_all(packed, AXES, 0, 0, axis_index_groups=order, tiled=True)
    pair = groups == 2
    done = pl.pallas_call(
        attend_pair_kernel if pair else functools.partial(attend_kernel, groups),
        out_shape=jax.ShapeDtypeStruct((slots, rows, size), jnp.bfloat16),
        in_specs=[vmem if pair else smem, vmem],
        out_specs=vmem,
        compiler_params=params,
    )(span_index, whole)
    back = lax.all_to_all(done, AXES, 0, 0, axis_index_groups=order, tiled=True)
    return pl.pallas_call(
        functools.partial(unpack_kernel, places),
        out_shape=jax.ShapeDtypeStruct((1, rows, width), jnp.bfloat16),
        in_specs=[vmem],
        out_specs=vmem,
        compiler_params=params,
    )(back)


def solution(mesh):
    spec = P("span", "seq", None)
    body = functools.partial(shards, mesh.shape["span"], mesh.shape["seq"])
    return jax.shard_map(body, mesh=mesh, in_specs=(spec, spec, spec, P()), out_specs=spec, check_vma=False)
```

```python
import functools
import math

import jax
import jax.numpy as jnp
from jax import lax
from jax.experimental import pallas as pl
from jax.experimental.pallas import tpu as pltpu
from jax.sharding import PartitionSpec as P

HEADS = 20
MASKED = -1e30
AXES = ("span", "seq")


def slot_heads(slots):
    spread = [d for d in range(slots) if d % 2 == 0] + [d for d in range(slots) if d % 2]
    heads = [0] * slots
    for place, d in enumerate(spread):
        heads[d] = place % HEADS
    return heads, spread[:HEADS]


def rank_order(groups, ranks):
    per = [r for c in range(2) for y in range(2) for r in range(ranks) if r % 4 == 2 * y + c]
    return [g * ranks + r for g in range(groups) for r in per]


def pack_kernel(heads, q_hbm, k_hbm, v_hbm, span_hbm, out_ref, bias_ref, held, spans, sems):
    copies = [
        pltpu.make_async_copy(src, held.at[pl.ds(i, 1)], sems.at[i])
        for i, src in enumerate((q_hbm, k_hbm, v_hbm))
    ]
    index = pltpu.make_async_copy(span_hbm, spans, sems.at[3])
    index.start()
    for c in copies:
        c.start()
    size = out_ref.shape[-1]
    for i, c in enumerate(copies):
        c.wait()
        for slot, head in enumerate(heads):
            out_ref[slot, i] = held[i, :, head * size:(head + 1) * size]
    index.wait()
    groups, tokens = bias_ref.shape
    key_group = lax.broadcasted_iota(jnp.int32, (1, tokens), 1) // (tokens // groups)
    for group in range(groups):
        seen = key_group == group
        for p in range(groups):
            seen |= (key_group == p) & (spans[p] == spans[group] - 1)
        bias_ref[group:group + 1] = jnp.where(seen, 0.0, MASKED)


def attend_kernel(groups, span_ref, in_ref, out_ref):
    slots, _, rows, size = in_ref.shape
    per = slots // groups
    tokens = per * rows
    scale = size ** -0.5

    def piece(part, group):
        block = in_ref[pl.ds(group * per, per), part].astype(jnp.float32)
        return block.reshape(tokens, size).astype(jnp.bfloat16)

    def one(group, carry):
        mine = span_ref[group]
        source = jnp.int32(0)
        found = jnp.int32(0)
        for p in range(groups):
            hit = (span_ref[p] == mine - 1).astype(jnp.int32)
            source = source + hit * p
            found = found + hit
        has = found > 0
        q = piece(0, group)
        dims = (((1,), (1,)), ((), ()))
        own = lax.dot_general(q, piece(1, group), dims, preferred_element_type=jnp.float32) * scale
        before = lax.dot_general(q, piece(1, source), dims, preferred_element_type=jnp.float32) * scale
        before = jnp.where(has, before, -1e30)
        top = jnp.maximum(jnp.max(own, -1, keepdims=True), jnp.max(before, -1, keepdims=True))
        own_w = jnp.exp(own - top)
        before_w = jnp.where(has, jnp.exp(before - top), 0.0)
        total = jnp.sum(own_w, -1, keepdims=True) + jnp.sum(before_w, -1, keepdims=True)
        acc = jnp.dot(own_w.astype(jnp.bfloat16), piece(2, group), preferred_element_type=jnp.float32)
        acc += jnp.dot(before_w.astype(jnp.bfloat16), piece(2, source), preferred_element_type=jnp.float32)
        result = (acc / total).reshape(per, rows, size).astype(jnp.bfloat16)
        out_ref[pl.ds(group * per, per)] = result
        return carry

    lax.fori_loop(0, groups, one, 0)


def attend_pair_kernel(bias_ref, in_ref, out_ref):
    slots, _, rows, size = in_ref.shape
    half = slots * rows // 2

    def piece(part):
        return in_ref[:, part].reshape(-1, size)

    scores = lax.dot_general(
        piece(0), piece(1), (((1,), (1,)), ((), ())), preferred_element_type=jnp.float32
    )
    scores = jnp.concatenate([scores[:half] + bias_ref[0:1], scores[half:] + bias_ref[1:2]], 0)
    scale = size ** -0.5 * math.log2(math.e)
    weights = jnp.exp2((scores - jnp.max(scores, -1, keepdims=True)) * scale)
    values = jnp.concatenate([piece(2), jnp.ones((slots * rows, size), jnp.bfloat16)], 1)
    acc = jnp.dot(weights.astype(jnp.bfloat16), values, preferred_element_type=jnp.float32)
    out_ref[...] = (acc[:, :size] / acc[:, size:]).reshape(slots, rows, size).astype(jnp.bfloat16)


def unpack_kernel(places, in_ref, out_ref):
    size = in_ref.shape[-1]
    for head, slot in enumerate(places):
        out_ref[0, :, head * size:(head + 1) * size] = in_ref[slot]


def shards(groups, ranks, queries, keys, values, span_index):
    rows, width = queries.shape[1:]
    size = width // HEADS
    slots = groups * ranks
    heads, places = slot_heads(slots)
    order = [rank_order(groups, ranks)] if ranks % 4 == 0 else None
    vmem = pl.BlockSpec(memory_space=pltpu.VMEM)
    smem = pl.BlockSpec(memory_space=pltpu.SMEM)
    hbm = pl.BlockSpec(memory_space=pltpu.HBM)
    queries, keys, values = [
        pltpu.with_memory_space_constraint(a, pltpu.HBM) for a in (queries, keys, values)
    ]
    params = pltpu.CompilerParams(vmem_limit_bytes=32 * 2**20)
    span_index = pltpu.with_memory_space_constraint(span_index, pltpu.HBM)
    packed, bias = pl.pallas_call(
        functools.partial(pack_kernel, heads),
        out_shape=[
            jax.ShapeDtypeStruct((slots, 3, rows, size), jnp.bfloat16),
            jax.ShapeDtypeStruct((groups, slots * rows), jnp.float32),
        ],
        in_specs=[hbm] * 4,
        out_specs=[vmem] * 2,
        scratch_shapes=[
            pltpu.VMEM((3, rows, width), jnp.bfloat16),
            pltpu.SMEM((groups,), jnp.int32),
            pltpu.SemaphoreType.DMA((4,)),
        ],
        compiler_params=params,
    )(queries, keys, values, span_index)
    whole = lax.all_to_all(packed, AXES, 0, 0, axis_index_groups=order, tiled=True)
    pair = groups == 2
    done = pl.pallas_call(
        attend_pair_kernel if pair else functools.partial(attend_kernel, groups),
        out_shape=jax.ShapeDtypeStruct((slots, rows, size), jnp.bfloat16),
        in_specs=[vmem if pair else smem, vmem],
        out_specs=vmem,
        compiler_params=params,
    )(bias if pair else span_index, whole)
    back = lax.all_to_all(done, AXES, 0, 0, axis_index_groups=order, tiled=True)
    return pl.pallas_call(
        functools.partial(unpack_kernel, places),
        out_shape=jax.ShapeDtypeStruct((1, rows, width), jnp.bfloat16),
        in_specs=[vmem],
        out_specs=vmem,
        compiler_params=params,
    )(back)


def solution(mesh):
    spec = P("span", "seq", None)
    body = functools.partial(shards, mesh.shape["span"], mesh.shape["seq"])
    return jax.shard_map(body, mesh=mesh, in_specs=(spec, spec, spec, P()), out_specs=spec, check_vma=False)
```
